256 devices in a mesh: seq: 32 (over x, z), dp: 8 (over y, core).
Axes of the slice: x: 4, y: 4, z: 8, core: 2. Of those that a mesh axis runs over, the one named last changes fastest.
Arguments:
- hidden_in: bfloat16 [8, 4096, 4096], P('dp', 'seq'), may hold values from -6 to 6
- queries: bfloat16 [8, 4096, 4096], P('dp', 'seq'), may hold values from -12 to 12, as said below
- keys: bfloat16 [8, 4096, 1024], P('dp', 'seq'), may hold values from -9 to 9, as said below
- values: bfloat16 [8, 4096, 1024], P('dp', 'seq'), may hold values from -6 to 6
- attn_out: bfloat16 [8, 4096, 4096], P('dp', 'seq'), may hold values from -6 to 6
- out_grad: bfloat16 [8, 4096, 4096], P('dp', 'seq'), may hold values from -1.1953125 to 1.1953125
- log_totals: float32 [8, 4096, 32], P('dp', 'seq'), as said below
Outputs:
- query_grad: bfloat16 [8, 4096, 4096], P('dp', 'seq')
- key_grad: bfloat16 [8, 4096, 1024], P('dp', 'seq')
- value_grad: bfloat16 [8, 4096, 1024], P('dp', 'seq')
- weight_grad: float32 [4096, 1024], P(('seq', 'dp'))
The draws below stay inside these ranges and needn't reach their ends.
Inputs may be any that keep to these rules, and one draw needn't show every extreme that they name: queries drawn independently. keys drawn independently. `log_totals`: the log-sum-exp, over keys at or before the query's position in the same trajectory, of that query head's scores as defined in the reference program.
All inputs are finite; a program needn't handle non-finite values.
Results may differ from the reference program's by a relative error of at most 0.0049.
Values may be sent and summed in bfloat16 or wider, within the bound.
A program may use at most 192 MiB of HBM per device.

```python
import jax
import jax.numpy as jnp
from jax import lax

D = 4096
HEADS = 32
KV_HEADS = 8
HEAD_DIM = 128
DOCS = 2
BATCH = 8
SEQ_LEN = 4096


def draw_common(key):
    query_seed = jax.random.fold_in(key, 101)
    key_seed = jax.random.fold_in(key, 202)
    query_draw = jnp.clip(2.0 * jax.random.normal(query_seed, (BATCH, SEQ_LEN, HEADS * HEAD_DIM), jnp.float32), -12.0, 12.0).astype(jnp.bfloat16)
    key_draw = jnp.clip(1.5 * jax.random.normal(key_seed, (BATCH, SEQ_LEN, KV_HEADS * HEAD_DIM), jnp.float32), -9.0, 9.0).astype(jnp.bfloat16)
    return (query_draw, key_draw)


def draw_queries(key, part):
    return draw_common(key)[0]


def draw_keys(key, part):
    return draw_common(key)[1]


def draw_log_totals(key, part):
    query_draw, key_draw = draw_common(key)
    groups = HEADS // KV_HEADS
    score_scale = HEAD_DIM ** (-0.5)
    doc_len = SEQ_LEN // DOCS
    query_wide = query_draw.astype(jnp.float32).reshape(BATCH, SEQ_LEN, KV_HEADS, groups, HEAD_DIM).transpose(0, 2, 3, 1, 4).reshape(BATCH * KV_HEADS, groups, SEQ_LEN, HEAD_DIM)
    key_wide = key_draw.astype(jnp.float32).reshape(BATCH, SEQ_LEN, KV_HEADS, HEAD_DIM).transpose(0, 2, 1, 3).reshape(BATCH * KV_HEADS, SEQ_LEN, HEAD_DIM)
    rows_at = jnp.arange(SEQ_LEN)[:, None]
    cols_at = jnp.arange(SEQ_LEN)[None, :]
    allowed = (rows_at >= cols_at) & (rows_at // doc_len == cols_at // doc_len)

    def one_group(operands):
        query_group, key_head = operands
        scores = jnp.einsum('gqd,kd->gqk', query_group, key_head, precision=lax.Precision.HIGHEST) * score_scale
        scores = jnp.where(allowed[None], scores, -1e+30)
        return jax.nn.logsumexp(scores, axis=2)
    totals = lax.map(one_group, (query_wide, key_wide))
    return totals.reshape(BATCH, KV_HEADS, groups, SEQ_LEN).transpose(0, 3, 1, 2).reshape(BATCH, SEQ_LEN, HEADS)


def spiked(values, key, source, target, parts, factor):
    owner, partner = [(jnp.arange(values.shape[dim]) // (values.shape[dim] // parts)).reshape([-1 if axis == dim else 1 for axis in range(values.ndim)]) for dim in (source, target)]
    chosen = jax.random.permutation(key, parts)[partner]
    strong = (owner == chosen) | (owner == (partner + parts // 2) % parts)
    return jnp.where(strong, factor * values, values)


def steps_of(stream_key, dims, pieces, smallest, top_value):
    def one(dim, blocks):
        steps = jax.random.uniform(jax.random.fold_in(jax.random.fold_in(stream_key, 6), dim), (blocks,), jnp.float32, smallest / len(pieces), top_value / len(pieces))
        return jnp.repeat(jnp.exp(steps), dims[dim] // blocks).reshape((-1,) + (1,) * (len(dims) - dim - 1))

    loudness = one(*pieces[0])
    for cut in pieces[1:]:
        loudness = loudness * one(*cut)
    return loudness


def scatter_about(stream_key, extent, scale, reach, split=(), dtype=jnp.bfloat16):
    drawn = scale * jax.random.normal(stream_key, extent, jnp.float32)
    if split:
        drawn = drawn * steps_of(stream_key, extent, split, -0.22, 0.18)
    return jnp.clip(drawn, -reach, reach).astype(dtype)


def bell_draw_with(key, shape, spread, limit, pieces, heavy, kind=jnp.bfloat16):
    values = spread * jax.random.normal(key, shape, jnp.float32)
    if pieces:
        values = values * steps_of(key, shape, pieces, -0.22, 0.18)
    return jnp.clip(spiked(values, jax.random.fold_in(key, 3), *heavy), -limit, limit).astype(kind)


def setup_inputs(seed: int = 0) -> dict:
    key_list = jax.random.split(jax.random.key(seed), 8)
    return {
        "hidden_in": bell_draw_with(key_list[0], (BATCH, SEQ_LEN, D), 1.0, 6.0, ((0, 8), (1, 32)), (1, 2, 32, 2.75)),
        "queries": draw_queries(jax.random.fold_in(key_list[7], 71), 0),
        "keys": draw_keys(jax.random.fold_in(key_list[7], 71), 0),
        "values": scatter_about(key_list[3], (BATCH, SEQ_LEN, KV_HEADS * HEAD_DIM), 1.0, 6.0, ((0, 8), (1, 32))),
        "attn_out": scatter_about(key_list[4], (BATCH, SEQ_LEN, HEADS * HEAD_DIM), 1.0, 6.0, ((0, 8), (1, 32))),
        "out_grad": scatter_about(key_list[5], (BATCH, SEQ_LEN, HEADS * HEAD_DIM), 0.2, 1.1953125, ((0, 8), (1, 32))),
        "log_totals": draw_log_totals(jax.random.fold_in(key_list[7], 71), 0),
    }


def lower_copy(array):
    return lax.optimization_barrier(array.astype(jnp.bfloat16)).astype(jnp.float32)


def group_backward(operands):
    query_group, key_head, value_head, grad_group, total_group, delta_group = operands
    length = key_head.shape[0]
    doc_len = length // DOCS
    block = min(512, doc_len)
    score_scale = HEAD_DIM ** -0.5
    keys_wide = key_head.astype(jnp.float32)
    values_wide = value_head.astype(jnp.float32)
    query_rows = []
    key_rows = []
    value_rows = []
    for trajectory in range(DOCS):
        base_row = trajectory * doc_len
        key_accum = jnp.zeros((doc_len, HEAD_DIM), jnp.float32)
        value_accum = jnp.zeros((doc_len, HEAD_DIM), jnp.float32)
        for position in range(doc_len // block):
            start_row = base_row + position * block
            end_row = start_row + block
            local_end = end_row - base_row
            query_block = query_group[:, start_row:end_row].astype(jnp.float32)
            grad_block = grad_group[:, start_row:end_row].astype(jnp.float32)
            key_front = keys_wide[base_row:end_row]
            value_front = values_wide[base_row:end_row]
            scores = jnp.einsum("gqd,kd->gqk", query_block, key_front) * score_scale
            causal = (start_row + jnp.arange(block))[:, None] >= (base_row + jnp.arange(local_end))[None, :]
            probs = jnp.where(causal[None], jnp.exp(scores - total_group[:, start_row:end_row, None]), 0.0)
            probs_low = lower_copy(probs)
            value_accum = value_accum.at[:local_end].add(jnp.einsum("gqk,gqd->kd", probs_low, grad_block))
            dprobs = jnp.einsum("gqd,kd->gqk", grad_block, value_front)
            dscores = probs * (dprobs - delta_group[:, start_row:end_row, None])
            dscores_low = lower_copy(dscores)
            query_rows.append((jnp.einsum("gqk,kd->gqd", dscores_low, key_front) * score_scale).astype(jnp.bfloat16))
            key_accum = key_accum.at[:local_end].add(jnp.einsum("gqk,gqd->kd", dscores_low, query_block) * score_scale)
        key_rows.append(key_accum.astype(jnp.bfloat16))
        value_rows.append(value_accum.astype(jnp.bfloat16))
    return jnp.concatenate(query_rows, axis=1), jnp.concatenate(key_rows, axis=0), jnp.concatenate(value_rows, axis=0)


def reference(hidden_in, queries, keys, values, attn_out, out_grad, log_totals):
    groups = HEADS // KV_HEADS
    row_delta = jnp.sum((out_grad.astype(jnp.float32) * attn_out.astype(jnp.float32)).reshape(BATCH, SEQ_LEN, HEADS, HEAD_DIM), axis=3)

    def by_group(array):
        shaped = array.reshape(BATCH, SEQ_LEN, KV_HEADS, groups, HEAD_DIM)
        return shaped.transpose(0, 2, 3, 1, 4).reshape(BATCH * KV_HEADS, groups, SEQ_LEN, HEAD_DIM)

    def by_head(array):
        shaped = array.reshape(BATCH, SEQ_LEN, KV_HEADS, HEAD_DIM)
        return shaped.transpose(0, 2, 1, 3).reshape(BATCH * KV_HEADS, SEQ_LEN, HEAD_DIM)

    def rows_group(array):
        shaped = array.reshape(BATCH, SEQ_LEN, KV_HEADS, groups)
        return shaped.transpose(0, 2, 3, 1).reshape(BATCH * KV_HEADS, groups, SEQ_LEN)

    query_part, key_part, value_part = lax.map(group_backward, (by_group(queries), by_head(keys), by_head(values), by_group(out_grad), rows_group(log_totals), rows_group(row_delta)))
    query_grad = query_part.reshape(BATCH, KV_HEADS, groups, SEQ_LEN, HEAD_DIM).transpose(0, 3, 1, 2, 4).reshape(BATCH, SEQ_LEN, HEADS * HEAD_DIM)
    key_grad = key_part.reshape(BATCH, KV_HEADS, SEQ_LEN, HEAD_DIM).transpose(0, 2, 1, 3).reshape(BATCH, SEQ_LEN, KV_HEADS * HEAD_DIM)
    value_grad = value_part.reshape(BATCH, KV_HEADS, SEQ_LEN, HEAD_DIM).transpose(0, 2, 1, 3).reshape(BATCH, SEQ_LEN, KV_HEADS * HEAD_DIM)
    weight_grad = jnp.dot(hidden_in.reshape(BATCH * SEQ_LEN, D).T, value_grad.reshape(BATCH * SEQ_LEN, KV_HEADS * HEAD_DIM), preferred_element_type=jnp.float32)
    return query_grad, key_grad, value_grad, weight_grad
```

```python
import functools

import jax
import jax.numpy as jnp
from jax import lax
from jax.experimental import pallas as pl
from jax.experimental.pallas import tpu as pltpu
from jax.sharding import PartitionSpec as P

HEADS = 32
KV_HEADS = 8
HEAD_DIM = 128
DOCS = 2
SCALE = HEAD_DIM ** (-0.5)
LOG2E = 1.4426950408889634
ROWS = 128
UNITS = 16
NT = (((1,), (1,)), ((), ()))
TN = (((0,), (0,)), ((), ()))
NN = (((1,), (0,)), ((), ()))
MESH = pl.DeviceIdType.MESH
ANY = pl.BlockSpec(memory_space=pl.ANY)
VMEM = pl.BlockSpec(memory_space=pltpu.VMEM)
DMA = pltpu.SemaphoreType.DMA


def place():
    seq = lax.axis_index("seq")
    unit = lax.rem(seq, UNITS)
    return seq, seq - unit, unit, unit // 8, lax.rem(unit, 8)


def send(src, dst, send_sem, recv_sem, **device):
    copy = pltpu.make_async_remote_copy(
        src_ref=src,
        dst_ref=dst,
        send_sem=send_sem,
        recv_sem=recv_sem,
        device_id=device,
        device_id_type=MESH,
    )
    copy.start()


def drain(ref, sem):
    pltpu.make_async_copy(ref, ref, sem).wait()


def rows_of(block):
    return pl.ds(pl.multiple_of(block * ROWS, ROWS), ROWS)


def columns_of(block, width=HEAD_DIM):
    return pl.ds(pl.multiple_of(block * width, width), width)


def exchange_kernel(
    query_ref,
    grad_ref,
    key_ref,
    value_ref,
    small_ref,
    hidden_ref,
    query_unit,
    grad_unit,
    key_unit,
    value_unit,
    small_unit,
    hidden_unit,
    own_sem,
    ring_send,
    ring_recv,
    pass_send,
    pass_recv,
    bulk_send,
    bulk_recv,
):
    seq, base, unit, half, lane = place()
    dp = lax.axis_index("dp")
    barrier = pltpu.get_barrier_semaphore()
    for step in range(1, UNITS):
        pl.semaphore_signal(
            barrier,
            inc=1,
            device_id={"seq": base + lax.rem(unit + step, UNITS)},
            device_id_type=MESH,
        )
    for step in range(1, 8):
        pl.semaphore_signal(
            barrier, inc=1, device_id={"dp": lax.rem(dp + step, 8)}, device_id_type=MESH
        )
    pl.semaphore_wait(barrier, 22)

    partner = base + (1 - half) * 8 + lane
    pairs = ((key_ref, key_unit), (value_ref, value_unit))
    for step in range(1, 8):
        target = lax.rem(lane + step, 8)
        for which, (source, landing) in enumerate(pairs):
            send(
                source.at[:, columns_of(target)],
                landing.at[rows_of(unit)],
                ring_send.at[which],
                ring_recv.at[which, lane],
                seq=base + half * 8 + target,
            )
    for which, (source, landing) in enumerate(pairs):
        send(
            source.at[:, columns_of(lane)],
            landing.at[rows_of(unit)],
            pass_send.at[which],
            pass_recv.at[which],
            seq=partner,
        )
    for step in range(1, UNITS):
        target = lax.rem(unit + step, UNITS)
        heads = lax.rem(target, 8) * 2 + target // 8
        send(
            query_ref.at[:, columns_of(heads, 256)],
            query_unit.at[rows_of(unit)],
            bulk_send.at[0],
            bulk_recv.at[0],
            seq=base + target,
        )
        send(
            grad_ref.at[:, columns_of(heads, 256)],
            grad_unit.at[rows_of(unit)],
            bulk_send.at[1],
            bulk_recv.at[1],
            seq=base + target,
        )
        send(
            small_ref.at[target],
            small_unit.at[unit],
            bulk_send.at[2],
            bulk_recv.at[2],
            seq=base + target,
        )
    for step in range(1, 8):
        target = lax.rem(dp + step, 8)
        send(
            hidden_ref.at[:, columns_of(target, 512)],
            hidden_unit.at[dp],
            bulk_send.at[3],
            bulk_recv.at[3],
            dp=target,
        )
    mine = lane * 2 + half
    own = (
        (key_ref.at[:, columns_of(lane)], key_unit.at[rows_of(unit)]),
        (value_ref.at[:, columns_of(lane)], value_unit.at[rows_of(unit)]),
        (query_ref.at[:, columns_of(mine, 256)], query_unit.at[rows_of(unit)]),
        (grad_ref.at[:, columns_of(mine, 256)], grad_unit.at[rows_of(unit)]),
        (small_ref.at[unit], small_unit.at[unit]),
        (hidden_ref.at[:, columns_of(dp, 512)], hidden_unit.at[dp]),
    )
    own = [pltpu.make_async_copy(*pair, own_sem.at[i]) for i, pair in enumerate(own)]
    for copy in own:
        copy.start()
    for step in range(1, 8):
        source = lax.rem(lane - step + 8, 8)
        for which, (_, landing) in enumerate(pairs):
            block = landing.at[rows_of(half * 8 + source)]
            drain(block, ring_recv.at[which, source])
            send(block, block, pass_send.at[which], pass_recv.at[which], seq=partner)
    for copy in own:
        copy.wait()
    for which, (_, landing) in enumerate(pairs):
        drain(landing.at[pl.ds(0, 7 * ROWS)], ring_send.at[which])
        drain(landing.at[pl.ds(0, 8 * ROWS)], pass_send.at[which])
        drain(landing.at[pl.ds(0, 8 * ROWS)], pass_recv.at[which])
    landings = (
        query_unit.at[pl.ds(0, 15 * ROWS)],
        grad_unit.at[pl.ds(0, 15 * ROWS)],
        small_unit.at[pl.ds(0, 15)],
        hidden_unit.at[pl.ds(0, 7)],
    )
    for i, landing in enumerate(landings):
        drain(landing, bulk_send.at[i])
        drain(landing, bulk_recv.at[i])


def exchange(queries, out_grad, keys, values, small, hidden):
    low = jnp.bfloat16
    return pl.pallas_call(
        exchange_kernel,
        out_shape=(
            jax.ShapeDtypeStruct((UNITS * ROWS, 256), low),
            jax.ShapeDtypeStruct((UNITS * ROWS, 256), low),
            jax.ShapeDtypeStruct((UNITS * ROWS, HEAD_DIM), low),
            jax.ShapeDtypeStruct((UNITS * ROWS, HEAD_DIM), low),
            jax.ShapeDtypeStruct((UNITS, 8, ROWS), jnp.float32),
            jax.ShapeDtypeStruct((8, ROWS, 512), low),
        ),
        in_specs=[ANY] * 6,
        out_specs=(ANY,) * 6,
        scratch_shapes=[
            DMA((6,)),
            DMA((2,)),
            DMA((2, 8)),
            DMA((2,)),
            DMA((2,)),
            DMA((4,)),
            DMA((4,)),
        ],
        compiler_params=pltpu.CompilerParams(collective_id=0, has_side_effects=True),
        name="exchange",
    )(queries, out_grad, keys, values, small, hidden)


def attention_kernel(
    query_ref,
    grad_ref,
    key_ref,
    value_ref,
    small_ref,
    query_out,
    key_out,
    value_out,
    key_low,
    value_low,
):
    block = 512
    per = block // ROWS
    key_out[...] = jnp.zeros_like(key_out)
    value_out[...] = jnp.zeros_like(value_out)
    causal = lax.broadcasted_iota(jnp.int32, (block, block), 0) <= lax.broadcasted_iota(
        jnp.int32, (block, block), 1
    )
    for position in range(query_ref.shape[0] // block):
        rows = slice(position * block, (position + 1) * block)
        for head in range(2):
            columns = slice(head * HEAD_DIM, (head + 1) * HEAD_DIM)
            query = query_ref[rows, columns]
            grad = grad_ref[rows, columns]
            total = jnp.concatenate(
                [small_ref[position * per + t, head : head + 1, :] for t in range(per)], axis=1
            )
            delta = jnp.concatenate(
                [small_ref[position * per + t, head + 2 : head + 3, :] for t in range(per)], axis=1
            )
            total = total * LOG2E
            query_sum = None
            for front in range(position + 1):
                fronts = slice(front * block, (front + 1) * block)
                key = key_ref[fronts, :]
                value = value_ref[fronts, :]
                scores = lax.dot_general(key, query, NT, preferred_element_type=jnp.float32)
                probs = jnp.exp2(scores * (SCALE * LOG2E) - total)
                if front == position:
                    probs = jnp.where(causal, probs, 0.0)
                dprobs = lax.dot_general(value, grad, NT, preferred_element_type=jnp.float32)
                value_out[fronts, :] += lax.dot_general(
                    probs.astype(jnp.bfloat16), grad, NN, preferred_element_type=jnp.float32
                )
                dscores = (probs * (dprobs - delta)).astype(jnp.bfloat16)
                key_out[fronts, :] += lax.dot_general(
                    dscores, query, NN, preferred_element_type=jnp.float32
                )
                step = lax.dot_general(dscores, key, TN, preferred_element_type=jnp.float32)
                query_sum = step if query_sum is None else query_sum + step
            query_out[rows, columns] = (query_sum * SCALE).astype(jnp.bfloat16)
    key_sum = key_out[...] * SCALE
    key_out[...] = key_sum
    key_low[...] = key_sum.astype(jnp.bfloat16)
    value_low[...] = value_out[...].astype(jnp.bfloat16)


def attention(query, grad, key, value, small):
    length = query.shape[0]
    narrow = (length, HEAD_DIM)
    return pl.pallas_call(
        attention_kernel,
        out_shape=(
            jax.ShapeDtypeStruct((length, 256), jnp.bfloat16),
            jax.ShapeDtypeStruct(narrow, jnp.float32),
            jax.ShapeDtypeStruct(narrow, jnp.float32),
            jax.ShapeDtypeStruct(narrow, jnp.bfloat16),
            jax.ShapeDtypeStruct(narrow, jnp.bfloat16),
        ),
        in_specs=[VMEM] * 5,
        out_specs=(VMEM,) * 5,
        compiler_params=pltpu.CompilerParams(vmem_limit_bytes=48 * 1024 * 1024),
        name="attention",
    )(query, grad, key, value, small)


def return_kernel(
    query_part,
    key_part,
    value_part,
    key_low,
    value_low,
    hidden_ref,
    query_grad,
    key_grad,
    value_grad,
    weight_grad,
    kept,
    halves,
    staged,
    gathered,
    product,
    product_in,
    summed,
    final_in,
    own_sem,
    kept_sem,
    half_send,
    half_recv,
    ring_send,
    ring_recv,
    query_send,
    query_recv,
    gather_send,
    gather_recv,
    core_send,
    core_recv,
    cross_send,
    cross_recv,
    final_send,
    final_recv,
):
    seq, base, unit, half, lane = place()
    dp = lax.axis_index("dp")
    across = seq // 8
    core = lax.rem(dp, 2)
    twin = dp + 1 - 2 * core
    owner = 4 * dp + across
    keeps = (owner == seq).astype(jnp.int32)
    barrier = pltpu.get_barrier_semaphore()
    for step in range(1, UNITS):
        pl.semaphore_signal(
            barrier,
            inc=1,
            device_id={"seq": base + lax.rem(unit + step, UNITS)},
            device_id_type=MESH,
        )
    for step in range(1, 4):
        pl.semaphore_signal(
            barrier,
            inc=1,
            device_id={"seq": lax.rem(across + step, 4) * 8 + lane},
            device_id_type=MESH,
        )
        pl.semaphore_signal(
            barrier, inc=1, device_id={"dp": lax.rem(dp + 2 * step, 8)}, device_id_type=MESH
        )
    pl.semaphore_signal(barrier, inc=1, device_id={"dp": twin}, device_id_type=MESH)
    for step in range(8):
        sender = lax.rem(seq, 4) * 8 + step
        outside = jnp.logical_or(sender != seq, seq // 4 != dp)

        @pl.when(outside)
        def _():
            pl.semaphore_signal(
                barrier,
                inc=1,
                device_id={"seq": sender, "dp": seq // 4},
                device_id_type=MESH,
            )

    pl.semaphore_wait(barrier, 30 - keeps)

    partner = base + (1 - half) * 8 + lane
    parts = ((value_part, value_low), (key_part, key_low))
    for which, (wide, low) in enumerate(parts):
        pltpu.make_async_copy(
            wide.at[pl.ds(pl.multiple_of(half * 8 * ROWS, ROWS), 8 * ROWS)],
            kept.at[which],
            kept_sem.at[which],
        ).start()
        for step in range(8):
            target = lax.rem(lane + 1 + step, 8)
            send(
                low.at[rows_of((1 - half) * 8 + target)],
                halves.at[which, target],
                half_send.at[which],
                half_recv.at[which, target],
                seq=partner,
            )
    for which in range(2):
        drain(kept.at[which], kept_sem.at[which])
        for step in range(8):
            target = lax.rem(lane + 1 + step, 8)
            drain(halves.at[which, target], half_recv.at[which, target])
            staged[which, target] = (
                kept[which, rows_of(target)] + halves[which, target].astype(jnp.float32)
            ).astype(jnp.bfloat16)
            landing = (gathered.at[dp] if which == 0 else key_grad).at[:, columns_of(lane)]
            if step < 7:
                send(
                    staged.at[which, target],
                    landing,
                    ring_send.at[which],
                    ring_recv.at[which],
                    seq=base + half * 8 + target,
                )
            else:
                pltpu.make_async_copy(staged.at[which, target], landing, own_sem.at[which]).start()
        if which == 0:
            mine = columns_of(lane * 2 + half, 256)
            for step in range(1, UNITS):
                target = lax.rem(unit + step, UNITS)
                send(
                    query_part.at[rows_of(target)],
                    query_grad.at[:, mine],
                    query_send,
                    query_recv,
                    seq=base + target,
                )
            pltpu.make_async_copy(
                query_part.at[rows_of(unit)], query_grad.at[:, mine], own_sem.at[2]
            ).start()

    drain(staged.at[0, 0], own_sem.at[0])
    drain(staged.at[0, pl.ds(0, 7)], ring_recv.at[0])
    block = gathered.at[dp]
    for step in (2, 1, 3):
        send(
            block,
            block,
            gather_send,
            gather_recv.at[dp // 2],
            dp=lax.rem(dp + 2 * step, 8),
        )
    send(block, block, core_send, core_recv, dp=twin)
    pltpu.make_async_copy(block, value_grad, own_sem.at[3]).start()
    for step in (1, 3, 2):
        source = lax.rem(dp + 2 * step, 8)
        arrived = gathered.at[source]
        drain(arrived, gather_recv.at[source // 2])
        send(arrived, arrived, core_send, core_recv, dp=twin)
    drain(gathered.at[pl.ds(0, 4)], core_recv)

    for step in range(4):
        target = lax.rem(across + 1 + step, 4)
        total = None
        for source in range(8):
            term = lax.dot_general(
                hidden_ref[source, :, columns_of(target)],
                gathered[source],
                TN,
                preferred_element_type=jnp.float32,
            )
            total = term if total is None else total + term
        if step < 3:
            product[target] = total.astype(jnp.bfloat16)
            send(
                product.at[target],
                product_in.at[across],
                cross_send,
                cross_recv,
                seq=target * 8 + lane,
            )
        else:
            summed[...] = total
    drain(product.at[pl.ds(0, 3)], cross_recv)
    for step in range(1, 4):
        summed[...] += product_in[lax.rem(across + step, 4)].astype(jnp.float32)
    for step in range(8):
        target = lax.rem(dp + step, 8)
        piece = summed.at[pl.ds(pl.multiple_of(target * 16, 16), 16)]
        landing = final_in.at[lane]
        if step == 0:

            @pl.when(keeps == 0)
            def _():
                send(
                    piece, landing, final_send.at[step], final_recv.at[lane], seq=owner, dp=target
                )

            @pl.when(keeps == 1)
            def _():
                pltpu.make_async_copy(piece, landing, final_recv.at[lane]).start()

        else:
            send(piece, landing, final_send.at[step], final_recv.at[lane], seq=owner, dp=target)
    for step in range(8):
        drain(final_in.at[step], final_recv.at[step])
        if step < 7:
            drain(final_in.at[step], final_send.at[step + 1])

    @pl.when(keeps == 0)
    def _():
        drain(final_in.at[0], final_send.at[0])

    total = final_in[0]
    for step in range(1, 8):
        total = total + final_in[step]
    weight_grad[...] = total

    drain(staged.at[1, 0], own_sem.at[1])
    drain(query_part.at[rows_of(0)], own_sem.at[2])
    drain(gathered.at[0], own_sem.at[3])
    drain(staged.at[1, pl.ds(0, 7)], ring_recv.at[1])
    drain(query_part.at[pl.ds(0, 15 * ROWS)], query_recv)
    drain(query_part.at[pl.ds(0, 15 * ROWS)], query_send)
    for which in range(2):
        drain(halves.at[which], half_send.at[which])
        drain(staged.at[which, pl.ds(0, 7)], ring_send.at[which])
    drain(gathered.at[pl.ds(0, 3)], gather_send)
    drain(gathered.at[pl.ds(0, 4)], core_send)
    drain(product.at[pl.ds(0, 3)], cross_send)


def give_back(query_part, key_part, value_part, key_low, value_low, hidden):
    low = jnp.bfloat16
    wide = jnp.float32
    return pl.pallas_call(
        return_kernel,
        out_shape=(
            jax.ShapeDtypeStruct((ROWS, HEADS * HEAD_DIM), low),
            jax.ShapeDtypeStruct((ROWS, KV_HEADS * HEAD_DIM), low),
            jax.ShapeDtypeStruct((ROWS, KV_HEADS * HEAD_DIM), low),
            jax.ShapeDtypeStruct((16, KV_HEADS * HEAD_DIM), wide),
        ),
        in_specs=[ANY] * 5 + [VMEM],
        out_specs=(ANY, ANY, ANY, VMEM),
        scratch_shapes=[
            pltpu.VMEM((2, 8 * ROWS, HEAD_DIM), wide),
            pltpu.VMEM((2, 8, ROWS, HEAD_DIM), low),
            pltpu.VMEM((2, 8, ROWS, HEAD_DIM), low),
            pltpu.VMEM((8, ROWS, KV_HEADS * HEAD_DIM), low),
            pltpu.VMEM((4, ROWS, KV_HEADS * HEAD_DIM), low),
            pltpu.VMEM((4, ROWS, KV_HEADS * HEAD_DIM), low),
            pltpu.VMEM((ROWS, KV_HEADS * HEAD_DIM), wide),
            pltpu.VMEM((8, 16, KV_HEADS * HEAD_DIM), wide),
            DMA((4,)),
            DMA((2,)),
            DMA((2,)),
            DMA((2, 8)),
            DMA((2,)),
            DMA((2,)),
            DMA,
            DMA,
            DMA,
            DMA((4,)),
            DMA,
            DMA,
            DMA,
            DMA,
            DMA((8,)),
            DMA((8,)),
        ],
        compiler_params=pltpu.CompilerParams(
            collective_id=1, has_side_effects=True, vmem_limit_bytes=48 * 1024 * 1024
        ),
        name="give_back",
    )(query_part, key_part, value_part, key_low, value_low, hidden)


def body(hidden_in, queries, keys, values, attn_out, out_grad, log_totals):
    delta = jnp.sum(
        (out_grad[0].astype(jnp.float32) * attn_out[0].astype(jnp.float32)).reshape(
            ROWS, HEADS, HEAD_DIM
        ),
        axis=2,
    )

    def by_unit(array):
        return array.reshape(ROWS, 8, 2, 2).transpose(2, 1, 3, 0).reshape(UNITS, 2, ROWS)

    small = jnp.concatenate(
        [by_unit(log_totals[0]), by_unit(delta), jnp.zeros((UNITS, 4, ROWS), jnp.float32)], axis=1
    )
    query_unit, grad_unit, key_unit, value_unit, small_unit, hidden_unit = exchange(
        queries[0], out_grad[0], keys[0], values[0], small, hidden_in[0]
    )
    query_part, key_part, value_part, key_low, value_low = attention(
        query_unit, grad_unit, key_unit, value_unit, small_unit
    )
    query_grad, key_grad, value_grad, weight_grad = give_back(
        query_part, key_part, value_part, key_low, value_low, hidden_unit
    )
    return (query_grad[None], key_grad[None], value_grad[None], weight_grad)


def solution(mesh):
    rows = P("dp", "seq", None)
    return jax.shard_map(
        body,
        mesh=mesh,
        in_specs=(rows,) * 7,
        out_specs=(rows, rows, rows, P(("seq", "dp"), None)),
        check_vma=False,
    )
```

```python
import functools

import jax
import jax.numpy as jnp
from jax import lax
from jax.experimental import pallas as pl
from jax.experimental.pallas import tpu as pltpu
from jax.sharding import PartitionSpec as P

HEADS = 32
KV_HEADS = 8
HEAD_DIM = 128
DOCS = 2
SCALE = HEAD_DIM ** (-0.5)
LOG2E = 1.4426950408889634
ROWS = 128
UNITS = 16
NT = (((1,), (1,)), ((), ()))
TN = (((0,), (0,)), ((), ()))
NN = (((1,), (0,)), ((), ()))
MESH = pl.DeviceIdType.MESH
ANY = pl.BlockSpec(memory_space=pl.ANY)
VMEM = pl.BlockSpec(memory_space=pltpu.VMEM)
DMA = pltpu.SemaphoreType.DMA


def place():
    seq = lax.axis_index("seq")
    unit = lax.rem(seq, UNITS)
    return seq, seq - unit, unit, unit // 8, lax.rem(unit, 8)


def send(src, dst, send_sem, recv_sem, **device):
    copy = pltpu.make_async_remote_copy(
        src_ref=src,
        dst_ref=dst,
        send_sem=send_sem,
        recv_sem=recv_sem,
        device_id=device,
        device_id_type=MESH,
    )
    copy.start()


def drain(ref, sem):
    pltpu.make_async_copy(ref, ref, sem).wait()


def rows_of(block):
    return pl.ds(pl.multiple_of(block * ROWS, ROWS), ROWS)


def columns_of(block, width=HEAD_DIM):
    return pl.ds(pl.multiple_of(block * width, width), width)


def exchange_kernel(
    query_ref,
    grad_ref,
    key_ref,
    value_ref,
    small_ref,
    hidden_ref,
    query_unit,
    grad_unit,
    key_unit,
    value_unit,
    small_unit,
    hidden_unit,
    own_sem,
    ring_send,
    ring_recv,
    pass_send,
    pass_recv,
    bulk_send,
    bulk_recv,
    core_send,
    core_recv,
    hidden_recv,
):
    seq, base, unit, half, lane = place()
    dp = lax.axis_index("dp")
    twin = dp + 1 - 2 * lax.rem(dp, 2)
    barrier = pltpu.get_barrier_semaphore()
    for step in range(1, UNITS):
        pl.semaphore_signal(
            barrier,
            inc=1,
            device_id={"seq": base + lax.rem(unit + step, UNITS)},
            device_id_type=MESH,
        )
    for other in (lax.rem(dp + 2, 8), lax.rem(dp + 4, 8), lax.rem(dp + 6, 8), twin):
        pl.semaphore_signal(barrier, inc=1, device_id={"dp": other}, device_id_type=MESH)
    pl.semaphore_wait(barrier, 19)

    partner = base + (1 - half) * 8 + lane
    pairs = ((key_ref, key_unit), (value_ref, value_unit))
    for step in range(1, 8):
        target = lax.rem(lane + step, 8)
        for which, (source, landing) in enumerate(pairs):
            send(
                source.at[:, columns_of(target)],
                landing.at[rows_of(unit)],
                ring_send.at[which],
                ring_recv.at[which, lane],
                seq=base + half * 8 + target,
            )
    for which, (source, landing) in enumerate(pairs):
        send(
            source.at[:, columns_of(lane)],
            landing.at[rows_of(unit)],
            pass_send.at[which],
            pass_recv.at[which],
            seq=partner,
        )
    for step in (2, 1, 3):
        send(
            hidden_ref,
            hidden_unit.at[dp],
            bulk_send.at[3],
            hidden_recv.at[dp // 2],
            dp=lax.rem(dp + 2 * step, 8),
        )
    send(hidden_ref, hidden_unit.at[dp], core_send, core_recv, dp=twin)
    for step in range(1, UNITS):
        target = lax.rem(unit + step, UNITS)
        heads = lax.rem(target, 8) * 2 + target // 8
        send(
            query_ref.at[:, columns_of(heads, 256)],
            query_unit.at[rows_of(unit)],
            bulk_send.at[0],
            bulk_recv.at[0],
            seq=base + target,
        )
        send(
            grad_ref.at[:, columns_of(heads, 256)],
            grad_unit.at[rows_of(unit)],
            bulk_send.at[1],
            bulk_recv.at[1],
            seq=base + target,
        )
        send(
            small_ref.at[target],
            small_unit.at[unit],
            bulk_send.at[2],
            bulk_recv.at[2],
            seq=base + target,
        )
    mine = lane * 2 + half
    own = (
        (key_ref.at[:, columns_of(lane)], key_unit.at[rows_of(unit)]),
        (value_ref.at[:, columns_of(lane)], value_unit.at[rows_of(unit)]),
        (query_ref.at[:, columns_of(mine, 256)], query_unit.at[rows_of(unit)]),
        (grad_ref.at[:, columns_of(mine, 256)], grad_unit.at[rows_of(unit)]),
        (small_ref.at[unit], small_unit.at[unit]),
        (hidden_ref, hidden_unit.at[dp]),
    )
    own = [pltpu.make_async_copy(*pair, own_sem.at[i]) for i, pair in enumerate(own)]
    for copy in own:
        copy.start()
    for step in range(1, 8):
        source = lax.rem(lane - step + 8, 8)
        for which, (_, landing) in enumerate(pairs):
            block = landing.at[rows_of(half * 8 + source)]
            drain(block, ring_recv.at[which, source])
            send(block, block, pass_send.at[which], pass_recv.at[which], seq=partner)
    for step in (1, 3, 2):
        source = lax.rem(dp + 2 * step, 8)
        arrived = hidden_unit.at[source]
        drain(arrived, hidden_recv.at[source // 2])
        send(arrived, arrived, core_send, core_recv, dp=twin)
    for copy in own:
        copy.wait()
    for which, (_, landing) in enumerate(pairs):
        drain(landing.at[pl.ds(0, 7 * ROWS)], ring_send.at[which])
        drain(landing.at[pl.ds(0, 8 * ROWS)], pass_send.at[which])
        drain(landing.at[pl.ds(0, 8 * ROWS)], pass_recv.at[which])
    landings = (
        query_unit.at[pl.ds(0, 15 * ROWS)],
        grad_unit.at[pl.ds(0, 15 * ROWS)],
        small_unit.at[pl.ds(0, 15)],
    )
    for i, landing in enumerate(landings):
        drain(landing, bulk_send.at[i])
        drain(landing, bulk_recv.at[i])
    drain(hidden_unit.at[pl.ds(0, 3)], bulk_send.at[3])
    drain(hidden_unit.at[pl.ds(0, 4)], core_send)
    drain(hidden_unit.at[pl.ds(0, 4)], core_recv)


def exchange(queries, out_grad, keys, values, small, hidden):
    low = jnp.bfloat16
    return pl.pallas_call(
        exchange_kernel,
        out_shape=(
            jax.ShapeDtypeStruct((UNITS * ROWS, 256), low),
            jax.ShapeDtypeStruct((UNITS * ROWS, 256), low),
            jax.ShapeDtypeStruct((UNITS * ROWS, HEAD_DIM), low),
            jax.ShapeDtypeStruct((UNITS * ROWS, HEAD_DIM), low),
            jax.ShapeDtypeStruct((UNITS, 8, ROWS), jnp.float32),
            jax.ShapeDtypeStruct((8, ROWS, HEADS * HEAD_DIM), low),
        ),
        in_specs=[ANY] * 6,
        out_specs=(ANY,) * 6,
        scratch_shapes=[
            DMA((6,)),
            DMA((2,)),
            DMA((2, 8)),
            DMA((2,)),
            DMA((2,)),
            DMA((4,)),
            DMA((3,)),
            DMA,
            DMA,
            DMA((4,)),
        ],
        compiler_params=pltpu.CompilerParams(collective_id=0, has_side_effects=True),
        name="exchange",
    )(queries, out_grad, keys, values, small, hidden)


def attention_kernel(
    query_ref,
    grad_ref,
    key_ref,
    value_ref,
    small_ref,
    query_out,
    key_out,
    value_out,
    key_low,
    value_low,
):
    block = 512
    per = block // ROWS
    key_out[...] = jnp.zeros_like(key_out)
    value_out[...] = jnp.zeros_like(value_out)
    causal = lax.broadcasted_iota(jnp.int32, (block, block), 0) <= lax.broadcasted_iota(
        jnp.int32, (block, block), 1
    )
    for position in range(query_ref.shape[0] // block):
        rows = slice(position * block, (position + 1) * block)
        for head in range(2):
            columns = slice(head * HEAD_DIM, (head + 1) * HEAD_DIM)
            query = query_ref[rows, columns]
            grad = grad_ref[rows, columns]
            total = jnp.concatenate(
                [small_ref[position * per + t, head : head + 1, :] for t in range(per)], axis=1
            )
            delta = jnp.concatenate(
                [small_ref[position * per + t, head + 2 : head + 3, :] for t in range(per)], axis=1
            )
            total = total * LOG2E
            query_sum = None
            for front in range(position + 1):
                fronts = slice(front * block, (front + 1) * block)
                key = key_ref[fronts, :]
                value = value_ref[fronts, :]
                scores = lax.dot_general(key, query, NT, preferred_element_type=jnp.float32)
                probs = jnp.exp2(scores * (SCALE * LOG2E) - total)
                if front == position:
                    probs = jnp.where(causal, probs, 0.0)
                dprobs = lax.dot_general(value, grad, NT, preferred_element_type=jnp.float32)
                value_out[fronts, :] += lax.dot_general(
                    probs.astype(jnp.bfloat16), grad, NN, preferred_element_type=jnp.float32
                )
                dscores = (probs * (dprobs - delta)).astype(jnp.bfloat16)
                key_out[fronts, :] += lax.dot_general(
                    dscores, query, NN, preferred_element_type=jnp.float32
                )
                step = lax.dot_general(dscores, key, TN, preferred_element_type=jnp.float32)
                query_sum = step if query_sum is None else query_sum + step
            query_out[rows, columns] = (query_sum * SCALE).astype(jnp.bfloat16)
    key_sum = key_out[...] * SCALE
    key_out[...] = key_sum
    key_low[...] = key_sum.astype(jnp.bfloat16)
    value_low[...] = value_out[...].astype(jnp.bfloat16)


def attention(query, grad, key, value, small):
    length = query.shape[0]
    narrow = (length, HEAD_DIM)
    return pl.pallas_call(
        attention_kernel,
        out_shape=(
            jax.ShapeDtypeStruct((length, 256), jnp.bfloat16),
            jax.ShapeDtypeStruct(narrow, jnp.float32),
            jax.ShapeDtypeStruct(narrow, jnp.float32),
            jax.ShapeDtypeStruct(narrow, jnp.bfloat16),
            jax.ShapeDtypeStruct(narrow, jnp.bfloat16),
        ),
        in_specs=[VMEM] * 5,
        out_specs=(VMEM,) * 5,
        compiler_params=pltpu.CompilerParams(vmem_limit_bytes=48 * 1024 * 1024),
        name="attention",
    )(query, grad, key, value, small)


def return_kernel(
    query_part,
    key_part,
    value_part,
    key_low,
    value_low,
    hidden_ref,
    query_grad,
    key_grad,
    value_grad,
    weight_grad,
    kept,
    halves,
    staged,
    value_own,
    value_in,
    hidden,
    product,
    product_in,
    summed,
    piece,
    piece_in,
    final,
    final_in,
    own_sem,
    half_send,
    half_recv,
    ring_send,
    ring_recv,
    query_send,
    query_recv,
    gather_send,
    gather_recv,
    cross_send,
    cross_recv,
    piece_send,
    piece_recv,
    final_send,
    final_recv,
):
    seq, base, unit, half, lane = place()
    dp = lax.axis_index("dp")
    across = seq // 8
    barrier = pltpu.get_barrier_semaphore()
    for step in range(1, UNITS):
        pl.semaphore_signal(
            barrier,
            inc=1,
            device_id={"seq": base + lax.rem(unit + step, UNITS)},
            device_id_type=MESH,
        )
    for step in range(1, 4):
        pl.semaphore_signal(
            barrier,
            inc=1,
            device_id={"seq": lax.rem(across + step, 4) * 8 + lane},
            device_id_type=MESH,
        )
    for step in range(1, 8):
        pl.semaphore_signal(
            barrier, inc=1, device_id={"dp": lax.rem(dp + step, 8)}, device_id_type=MESH
        )
    pl.semaphore_wait(barrier, 25)

    partner = base + (1 - half) * 8 + lane
    parts = ((value_part, value_low), (key_part, key_low))
    for which, (wide, low) in enumerate(parts):
        pltpu.make_async_copy(
            wide.at[pl.ds(pl.multiple_of(half * 8 * ROWS, ROWS), 8 * ROWS)],
            kept.at[which],
            own_sem.at[which],
        ).start()
        for step in range(8):
            target = lax.rem(lane + 1 + step, 8)
            send(
                low.at[rows_of((1 - half) * 8 + target)],
                halves.at[which, target],
                half_send.at[which],
                half_recv.at[which, target],
                seq=partner,
            )
    pltpu.make_async_copy(hidden_ref, hidden, own_sem.at[2]).start()
    for which in range(2):
        drain(kept.at[which], own_sem.at[which])
        for step in range(8):
            target = lax.rem(lane + 1 + step, 8)
            drain(halves.at[which, target], half_recv.at[which, target])
            staged[which, target] = (
                kept[which, rows_of(target)] + halves[which, target].astype(jnp.float32)
            ).astype(jnp.bfloat16)
            landing = (value_own if which == 0 else key_grad).at[:, columns_of(lane)]
            if step < 7:
                send(
                    staged.at[which, target],
                    landing,
                    ring_send.at[which],
                    ring_recv.at[which],
                    seq=base + half * 8 + target,
                )
            else:
                pltpu.make_async_copy(
                    staged.at[which, target], landing, own_sem.at[3 + which]
                ).start()
        if which == 0:
            mine = columns_of(lane * 2 + half, 256)
            for step in range(1, UNITS):
                target = lax.rem(unit + step, UNITS)
                send(
                    query_part.at[rows_of(target)],
                    query_grad.at[:, mine],
                    query_send,
                    query_recv,
                    seq=base + target,
                )
            pltpu.make_async_copy(
                query_part.at[rows_of(unit)], query_grad.at[:, mine], own_sem.at[5]
            ).start()

    drain(staged.at[0, 0], own_sem.at[3])
    drain(staged.at[0, pl.ds(0, 7)], ring_recv.at[0])
    for step in range(1, 8):
        target = lax.rem(dp + step, 8)
        send(
            value_own.at[:, columns_of(target)],
            value_in.at[rows_of(dp)],
            gather_send,
            gather_recv,
            dp=target,
        )
    pltpu.make_async_copy(value_own, value_grad, own_sem.at[6]).start()
    value_in[rows_of(dp), :] = value_own[:, columns_of(dp)]
    drain(hidden, own_sem.at[2])
    drain(value_in.at[pl.ds(0, 7 * ROWS)], gather_recv)
    for step in range(4):
        target = lax.rem(across + 1 + step, 4)
        total = lax.dot_general(
            value_in[...],
            hidden[:, columns_of(target, 8 * ROWS)],
            TN,
            preferred_element_type=jnp.float32,
        )
        if step < 3:
            product[target] = total.astype(jnp.bfloat16)
            send(
                product.at[target],
                product_in.at[across],
                cross_send,
                cross_recv,
                seq=target * 8 + lane,
            )
        else:
            summed[...] = total
    drain(product.at[pl.ds(0, 3)], cross_recv)
    for step in range(8):
        target = lax.rem(lane + 1 + step, 8)
        columns = columns_of(target)
        total = summed[:, columns]
        for source in range(1, 4):
            total = total + product_in[lax.rem(across + source, 4), :, columns].astype(jnp.float32)
        if step < 7:
            piece[target] = total
            send(
                piece.at[target],
                piece_in.at[lane],
                piece_send,
                piece_recv,
                seq=across * 8 + target,
            )
        else:
            piece_in[lane] = total
    drain(piece.at[pl.ds(0, 7)], piece_recv)
    total = piece_in[0]
    for step in range(1, 8):
        total = total + piece_in[step]
    final[...] = total.T
    for step in range(1, 8):
        target = lax.rem(dp + step, 8)
        send(
            final.at[pl.ds(pl.multiple_of(target * 16, 16), 16)],
            final_in.at[:, columns_of(dp)],
            final_send,
            final_recv,
            dp=target,
        )
    final_in[:, columns_of(dp)] = final[pl.ds(pl.multiple_of(dp * 16, 16), 16), :]
    drain(final.at[pl.ds(0, 7 * 16)], final_recv)
    weight_grad[...] = final_in[...]

    drain(staged.at[1, 0], own_sem.at[4])
    drain(query_part.at[rows_of(0)], own_sem.at[5])
    drain(value_own, own_sem.at[6])
    drain(staged.at[1, pl.ds(0, 7)], ring_recv.at[1])
    drain(query_part.at[pl.ds(0, 15 * ROWS)], query_recv)
    drain(query_part.at[pl.ds(0, 15 * ROWS)], query_send)
    for which in range(2):
        drain(halves.at[which], half_send.at[which])
        drain(staged.at[which, pl.ds(0, 7)], ring_send.at[which])
    drain(value_in.at[pl.ds(0, 7 * ROWS)], gather_send)
    drain(product.at[pl.ds(0, 3)], cross_send)
    drain(piece.at[pl.ds(0, 7)], piece_send)
    drain(final.at[pl.ds(0, 7 * 16)], final_send)


def give_back(query_part, key_part, value_part, key_low, value_low, hidden):
    low = jnp.bfloat16
    wide = jnp.float32
    columns = KV_HEADS * HEAD_DIM
    return pl.pallas_call(
        return_kernel,
        out_shape=(
            jax.ShapeDtypeStruct((ROWS, HEADS * HEAD_DIM), low),
            jax.ShapeDtypeStruct((ROWS, columns), low),
            jax.ShapeDtypeStruct((ROWS, columns), low),
            jax.ShapeDtypeStruct((16, columns), wide),
        ),
        in_specs=[ANY] * 6,
        out_specs=(ANY, ANY, ANY, VMEM),
        scratch_shapes=[
            pltpu.VMEM((2, 8 * ROWS, HEAD_DIM), wide),
            pltpu.VMEM((2, 8, ROWS, HEAD_DIM), low),
            pltpu.VMEM((2, 8, ROWS, HEAD_DIM), low),
            pltpu.VMEM((ROWS, columns), low),
            pltpu.VMEM((8 * ROWS, HEAD_DIM), low),
            pltpu.VMEM((8 * ROWS, HEADS * HEAD_DIM), low),
            pltpu.VMEM((4, ROWS, columns), low),
            pltpu.VMEM((4, ROWS, columns), low),
            pltpu.VMEM((ROWS, columns), wide),
            pltpu.VMEM((8, ROWS, ROWS), wide),
            pltpu.VMEM((8, ROWS, ROWS), wide),
            pltpu.VMEM((ROWS, ROWS), wide),
            pltpu.VMEM((16, columns), wide),
            DMA((7,)),
            DMA((2,)),
            DMA((2, 8)),
            DMA((2,)),
            DMA((2,)),
            DMA,
            DMA,
            DMA,
            DMA,
            DMA,
            DMA,
            DMA,
            DMA,
            DMA,
            DMA,
        ],
        compiler_params=pltpu.CompilerParams(
            collective_id=1, has_side_effects=True, vmem_limit_bytes=48 * 1024 * 1024
        ),
        name="give_back",
    )(query_part, key_part, value_part, key_low, value_low, hidden)


def body(hidden_in, queries, keys, values, attn_out, out_grad, log_totals):
    delta = jnp.sum(
        (out_grad[0].astype(jnp.float32) * attn_out[0].astype(jnp.float32)).reshape(
            ROWS, HEADS, HEAD_DIM
        ),
        axis=2,
    )

    def by_unit(array):
        return array.reshape(ROWS, 8, 2, 2).transpose(2, 1, 3, 0).reshape(UNITS, 2, ROWS)

    small = jnp.concatenate(
        [by_unit(log_totals[0]), by_unit(delta), jnp.zeros((UNITS, 4, ROWS), jnp.float32)], axis=1
    )
    query_unit, grad_unit, key_unit, value_unit, small_unit, hidden_unit = exchange(
        queries[0], out_grad[0], keys[0], values[0], small, hidden_in[0]
    )
    query_part, key_part, value_part, key_low, value_low = attention(
        query_unit, grad_unit, key_unit, value_unit, small_unit
    )
    query_grad, key_grad, value_grad, weight_grad = give_back(
        query_part,
        key_part,
        value_part,
        key_low,
        value_low,
        hidden_unit.reshape(8 * ROWS, HEADS * HEAD_DIM),
    )
    return (query_grad[None], key_grad[None], value_grad[None], weight_grad)


def solution(mesh):
    rows = P("dp", "seq", None)
    return jax.shard_map(
        body,
        mesh=mesh,
        in_specs=(rows,) * 7,
        out_specs=(rows, rows, rows, P(("seq", "dp"), None)),
        check_vma=False,
    )
```

```python
import functools

import jax
import jax.numpy as jnp
from jax import lax
from jax.experimental import pallas as pl
from jax.experimental.pallas import tpu as pltpu
from jax.sharding import PartitionSpec as P

HEADS = 32
KV_HEADS = 8
HEAD_DIM = 128
DOCS = 2
SCALE = HEAD_DIM ** (-0.5)
LOG2E = 1.4426950408889634
BLOCK = 512
ROWS = 128
UNITS = 16
NT = (((1,), (1,)), ((), ()))
TN = (((0,), (0,)), ((), ()))
NN = (((1,), (0,)), ((), ()))
MESH = pl.DeviceIdType.MESH
ANY = pl.BlockSpec(memory_space=pl.ANY)
VMEM = pl.BlockSpec(memory_space=pltpu.VMEM)
DMA = pltpu.SemaphoreType.DMA


def place():
    seq = lax.axis_index("seq")
    unit = lax.rem(seq, UNITS)
    return seq, seq - unit, unit, unit // 8, lax.rem(unit, 8)


def send(src, dst, send_sem, recv_sem, **device):
    copy = pltpu.make_async_remote_copy(
        src_ref=src,
        dst_ref=dst,
        send_sem=send_sem,
        recv_sem=recv_sem,
        device_id=device,
        device_id_type=MESH,
    )
    copy.start()


def drain(ref, sem):
    pltpu.make_async_copy(ref, ref, sem).wait()


def rows_of(block):
    return pl.ds(pl.multiple_of(block * ROWS, ROWS), ROWS)


def columns_of(block, width=HEAD_DIM):
    return pl.ds(pl.multiple_of(block * width, width), width)


def scores_of(key, query, total):
    scores = lax.dot_general(key, query, NT, preferred_element_type=jnp.float32)
    return jnp.exp2(scores * (SCALE * LOG2E) - total)


def kernel(
    query_ref,
    grad_ref,
    key_ref,
    value_ref,
    small_ref,
    hidden_ref,
    query_grad,
    key_grad,
    value_grad,
    weight_grad,
    query_unit,
    grad_unit,
    key_unit,
    value_unit,
    small_unit,
    hidden_unit,
    probs_kept,
    query_part,
    key_sum,
    value_sum,
    low,
    halves,
    staged,
    value_own,
    value_in,
    product,
    product_in,
    summed,
    piece,
    piece_in,
    final,
    final_in,
    own_sem,
    front_send,
    front_recv,
    pass_send,
    pass_recv,
    bulk_send,
    bulk_recv,
    hidden_send,
    hidden_recv,
    core_send,
    core_recv,
    half_send,
    half_recv,
    ring_send,
    ring_recv,
    query_send,
    query_recv,
    gather_send,
    gather_recv,
    cross_send,
    cross_recv,
    piece_send,
    piece_recv,
    final_send,
    final_recv,
):
    seq, base, unit, half, lane = place()
    dp = lax.axis_index("dp")
    across = seq // 8
    twin = dp + 1 - 2 * lax.rem(dp, 2)
    partner = base + (1 - half) * 8 + lane
    barrier = pltpu.get_barrier_semaphore()
    for step in range(1, UNITS):
        pl.semaphore_signal(
            barrier,
            inc=1,
            device_id={"seq": base + lax.rem(unit + step, UNITS)},
            device_id_type=MESH,
        )
    for step in range(1, 4):
        pl.semaphore_signal(
            barrier,
            inc=1,
            device_id={"seq": lax.rem(across + step, 4) * 8 + lane},
            device_id_type=MESH,
        )
    for step in range(1, 8):
        pl.semaphore_signal(
            barrier, inc=1, device_id={"dp": lax.rem(dp + step, 8)}, device_id_type=MESH
        )
    pl.semaphore_wait(barrier, 25)

    pairs = ((key_ref, key_unit), (value_ref, value_unit))
    for step in range(1, 8):
        target = lax.rem(lane + step, 8)
        for which, (source, landing) in enumerate(pairs):
            send(
                source.at[:, columns_of(target)],
                landing.at[rows_of(unit)],
                front_send.at[which],
                front_recv.at[which, lane],
                seq=base + half * 8 + target,
            )
    for which, (source, landing) in enumerate(pairs):
        send(
            source.at[:, columns_of(lane)],
            landing.at[rows_of(unit)],
            pass_send.at[which],
            pass_recv.at[which],
            seq=partner,
        )
    for head in range(2):
        for step in range(1, UNITS):
            target = lax.rem(unit + step, UNITS)
            columns = columns_of(lax.rem(target, 8) * 4 + (target // 8) * 2 + head)
            for which, (source, landing) in enumerate(
                ((query_ref, query_unit), (grad_ref, grad_unit))
            ):
                send(
                    source.at[:, columns],
                    landing.at[head, rows_of(unit)],
                    bulk_send.at[head * 2 + which],
                    bulk_recv.at[head * 2 + which],
                    seq=base + target,
                )
            if head == 0:
                send(
                    small_ref.at[target],
                    small_unit.at[unit],
                    bulk_send.at[4],
                    bulk_recv.at[4],
                    seq=base + target,
                )
        if head == 0:
            for step in (2, 1, 3):
                send(
                    hidden_ref,
                    hidden_unit.at[rows_of(dp)],
                    hidden_send,
                    hidden_recv.at[dp // 2],
                    dp=lax.rem(dp + 2 * step, 8),
                )
            send(hidden_ref, hidden_unit.at[rows_of(dp)], core_send, core_recv, dp=twin)
    mine = lane * 4 + half * 2
    own = (
        (key_ref.at[:, columns_of(lane)], key_unit.at[rows_of(unit)]),
        (value_ref.at[:, columns_of(lane)], value_unit.at[rows_of(unit)]),
        (small_ref.at[unit], small_unit.at[unit]),
        (query_ref.at[:, columns_of(mine)], query_unit.at[0, rows_of(unit)]),
        (grad_ref.at[:, columns_of(mine)], grad_unit.at[0, rows_of(unit)]),
        (query_ref.at[:, columns_of(mine + 1)], query_unit.at[1, rows_of(unit)]),
        (grad_ref.at[:, columns_of(mine + 1)], grad_unit.at[1, rows_of(unit)]),
        (hidden_ref, hidden_unit.at[rows_of(dp)]),
    )
    own = [pltpu.make_async_copy(*pair, own_sem.at[i]) for i, pair in enumerate(own)]
    for copy in own:
        copy.start()
    for step in range(1, 8):
        source = lax.rem(lane - step + 8, 8)
        for which, (_, landing) in enumerate(pairs):
            block = landing.at[rows_of(half * 8 + source)]
            drain(block, front_recv.at[which, source])
            send(block, block, pass_send.at[which], pass_recv.at[which], seq=partner)

    key_sum[...] = jnp.zeros_like(key_sum)
    value_sum[...] = jnp.zeros_like(value_sum)
    causal = lax.broadcasted_iota(jnp.int32, (BLOCK, BLOCK), 0) <= lax.broadcasted_iota(
        jnp.int32, (BLOCK, BLOCK), 1
    )
    per = BLOCK // ROWS
    positions = UNITS * ROWS // BLOCK

    def spread(position, row):
        return jnp.concatenate(
            [small_unit[position * per + t, row : row + 1, :] for t in range(per)], axis=1
        )

    def later(head, position, front, probs, query, grad, delta):
        fronts = pl.ds(front * BLOCK, BLOCK)
        key = key_unit[fronts, :]
        dprobs = lax.dot_general(
            value_unit[fronts, :], grad, NT, preferred_element_type=jnp.float32
        )
        dscores = (probs * (dprobs - delta)).astype(jnp.bfloat16)
        key_sum[fronts, :] += lax.dot_general(
            dscores, query, NN, preferred_element_type=jnp.float32
        )
        return lax.dot_general(dscores, key, TN, preferred_element_type=jnp.float32)

    def first(position, front, query, grad, total):
        fronts = pl.ds(front * BLOCK, BLOCK)
        probs = scores_of(key_unit[fronts, :], query, total)
        if front == position:
            probs = jnp.where(causal, probs, 0.0)
        value_sum[fronts, :] += lax.dot_general(
            probs.astype(jnp.bfloat16), grad, NN, preferred_element_type=jnp.float32
        )
        return probs

    def give_query(head):
        for step in range(1, UNITS):
            target = lax.rem(unit + step, UNITS)
            send(
                query_part.at[head, rows_of(target)],
                query_grad.at[:, columns_of(mine + head)],
                query_send.at[head],
                query_recv.at[head],
                seq=base + target,
            )
        pltpu.make_async_copy(
            query_part.at[head, rows_of(unit)],
            query_grad.at[:, columns_of(mine + head)],
            own_sem.at[8 + head],
        ).start()

    for copy in own[:5]:
        copy.wait()
    for which, (_, landing) in enumerate(pairs):
        drain(landing.at[pl.ds(0, 8 * ROWS)], pass_recv.at[which])
    some = pl.ds(0, 15 * ROWS)
    drain(query_unit.at[0, some], bulk_recv.at[0])
    drain(grad_unit.at[0, some], bulk_recv.at[1])
    drain(small_unit.at[pl.ds(0, 15)], bulk_recv.at[4])
    for position in range(positions):
        rows = pl.ds(position * BLOCK, BLOCK)
        query = query_unit[0, rows, :]
        grad = grad_unit[0, rows, :]
        total = spread(position, 0) * LOG2E
        delta = spread(position, 2)
        query_sum = None
        for front in range(position + 1):
            probs = first(position, front, query, grad, total)
            term = later(0, position, front, probs, query, grad, delta)
            query_sum = term if query_sum is None else query_sum + term
        query_part[0, rows, :] = (query_sum * SCALE).astype(jnp.bfloat16)
    give_query(0)

    for step in (1, 3, 2):
        source = lax.rem(dp + 2 * step, 8)
        arrived = hidden_unit.at[rows_of(source)]
        drain(arrived, hidden_recv.at[source // 2])
        send(arrived, arrived, core_send, core_recv, dp=twin)

    for copy in own[5:7]:
        copy.wait()
    drain(query_unit.at[1, some], bulk_recv.at[2])
    drain(grad_unit.at[1, some], bulk_recv.at[3])
    slot = 0
    for position in range(positions):
        rows = pl.ds(position * BLOCK, BLOCK)
        query = query_unit[1, rows, :]
        grad = grad_unit[1, rows, :]
        total = spread(position, 1) * LOG2E
        for front in range(position + 1):
            probs_kept[slot] = first(position, front, query, grad, total)
            slot += 1

    def give_half(which, array, factor):
        for step in range(8):
            target = lax.rem(lane + 1 + step, 8)
            low[which, target] = (array[rows_of((1 - half) * 8 + target), :] * factor).astype(
                jnp.bfloat16
            )
            send(
                low.at[which, target],
                halves.at[which, target],
                half_send.at[which],
                half_recv.at[which, target],
                seq=partner,
            )

    def give_whole(which, array, factor, landing):
        landing = landing.at[:, columns_of(lane)]
        for step in range(8):
            target = lax.rem(lane + 1 + step, 8)
            drain(halves.at[which, target], half_recv.at[which, target])
            staged[which, target] = (
                array[rows_of(half * 8 + target), :] * factor
                + halves[which, target].astype(jnp.float32)
            ).astype(jnp.bfloat16)
            if step < 7:
                send(
                    staged.at[which, target],
                    landing,
                    ring_send.at[which],
                    ring_recv.at[which],
                    seq=base + half * 8 + target,
                )
            else:
                pltpu.make_async_copy(
                    staged.at[which, target], landing, own_sem.at[10 + which]
                ).start()

    give_half(0, value_sum, 1.0)
    slot = 0
    for position in range(positions):
        rows = pl.ds(position * BLOCK, BLOCK)
        query = query_unit[1, rows, :]
        grad = grad_unit[1, rows, :]
        delta = spread(position, 3)
        query_sum = None
        for front in range(position + 1):
            term = later(1, position, front, probs_kept[slot], query, grad, delta)
            query_sum = term if query_sum is None else query_sum + term
            slot += 1
        query_part[1, rows, :] = (query_sum * SCALE).astype(jnp.bfloat16)
    give_half(1, key_sum, SCALE)
    give_whole(0, value_sum, 1.0, value_own)
    give_query(1)
    give_whole(1, key_sum, SCALE, key_grad)

    drain(staged.at[0, 0], own_sem.at[10])
    drain(staged.at[0, pl.ds(0, 7)], ring_recv.at[0])
    for step in range(1, 8):
        target = lax.rem(dp + step, 8)
        send(
            value_own.at[:, columns_of(target)],
            value_in.at[rows_of(dp)],
            gather_send,
            gather_recv,
            dp=target,
        )
    pltpu.make_async_copy(value_own, value_grad, own_sem.at[12]).start()
    value_in[rows_of(dp), :] = value_own[:, columns_of(dp)]
    own[7].wait()
    drain(hidden_unit.at[pl.ds(0, 4 * ROWS)], core_recv)
    drain(value_in.at[pl.ds(0, 7 * ROWS)], gather_recv)
    for step in range(4):
        target = lax.rem(across + 1 + step, 4)
        total = lax.dot_general(
            value_in[...],
            hidden_unit[:, columns_of(target, 8 * ROWS)],
            TN,
            preferred_element_type=jnp.float32,
        )
        if step < 3:
            product[target] = total.astype(jnp.bfloat16)
            send(
                product.at[target],
                product_in.at[across],
                cross_send,
                cross_recv,
                seq=target * 8 + lane,
            )
        else:
            summed[...] = total
    drain(product.at[pl.ds(0, 3)], cross_recv)
    for step in range(8):
        target = lax.rem(lane + 1 + step, 8)
        columns = columns_of(target)
        total = summed[:, columns]
        for source in range(1, 4):
            total = total + product_in[lax.rem(across + source, 4), :, columns].astype(jnp.float32)
        if step < 7:
            piece[target] = total
            send(
                piece.at[target],
                piece_in.at[lane],
                piece_send,
                piece_recv,
                seq=across * 8 + target,
            )
        else:
            piece_in[lane] = total
    drain(piece.at[pl.ds(0, 7)], piece_recv)
    total = piece_in[0]
    for step in range(1, 8):
        total = total + piece_in[step]
    final[...] = total.T
    for step in range(1, 8):
        target = lax.rem(dp + step, 8)
        send(
            final.at[pl.ds(pl.multiple_of(target * 16, 16), 16)],
            final_in.at[:, columns_of(dp)],
            final_send,
            final_recv,
            dp=target,
        )
    final_in[:, columns_of(dp)] = final[pl.ds(pl.multiple_of(dp * 16, 16), 16), :]
    drain(final.at[pl.ds(0, 7 * 16)], final_recv)
    weight_grad[...] = final_in[...]

    for which, (_, landing) in enumerate(pairs):
        drain(landing.at[pl.ds(0, 7 * ROWS)], front_send.at[which])
        drain(landing.at[pl.ds(0, 8 * ROWS)], pass_send.at[which])
    for which in range(4):
        drain(query_unit.at[0, some], bulk_send.at[which])
    drain(small_unit.at[pl.ds(0, 15)], bulk_send.at[4])
    drain(hidden_unit.at[pl.ds(0, 3 * ROWS)], hidden_send)
    drain(hidden_unit.at[pl.ds(0, 4 * ROWS)], core_send)
    drain(staged.at[1, 0], own_sem.at[11])
    drain(value_own, own_sem.at[12])
    drain(staged.at[1, pl.ds(0, 7)], ring_recv.at[1])
    for head in range(2):
        drain(query_part.at[head, rows_of(0)], own_sem.at[8 + head])
        drain(query_part.at[head, some], query_recv.at[head])
        drain(query_part.at[head, some], query_send.at[head])
    for which in range(2):
        drain(halves.at[which], half_send.at[which])
        drain(staged.at[which, pl.ds(0, 7)], ring_send.at[which])
    drain(value_in.at[pl.ds(0, 7 * ROWS)], gather_send)
    drain(product.at[pl.ds(0, 3)], cross_send)
    drain(piece.at[pl.ds(0, 7)], piece_send)
    drain(final.at[pl.ds(0, 7 * 16)], final_send)


def backward(queries, out_grad, keys, values, small, hidden):
    low = jnp.bfloat16
    wide = jnp.float32
    columns = KV_HEADS * HEAD_DIM
    length = UNITS * ROWS
    positions = length // BLOCK
    slots = positions * (positions + 1) // 2
    return pl.pallas_call(
        kernel,
        out_shape=(
            jax.ShapeDtypeStruct((ROWS, HEADS * HEAD_DIM), low),
            jax.ShapeDtypeStruct((ROWS, columns), low),
            jax.ShapeDtypeStruct((ROWS, columns), low),
            jax.ShapeDtypeStruct((16, columns), wide),
        ),
        in_specs=[ANY] * 6,
        out_specs=(ANY, ANY, ANY, VMEM),
        scratch_shapes=[
            pltpu.VMEM((2, length, HEAD_DIM), low),
            pltpu.VMEM((2, length, HEAD_DIM), low),
            pltpu.VMEM((length, HEAD_DIM), low),
            pltpu.VMEM((length, HEAD_DIM), low),
            pltpu.VMEM((UNITS, 8, ROWS), wide),
            pltpu.VMEM((8 * ROWS, HEADS * HEAD_DIM), low),
            pltpu.VMEM((slots, BLOCK, BLOCK), wide),
            pltpu.VMEM((2, length, HEAD_DIM), low),
            pltpu.VMEM((length, HEAD_DIM), wide),
            pltpu.VMEM((length, HEAD_DIM), wide),
            pltpu.VMEM((2, 8, ROWS, HEAD_DIM), low),
            pltpu.VMEM((2, 8, ROWS, HEAD_DIM), low),
            pltpu.VMEM((2, 8, ROWS, HEAD_DIM), low),
            pltpu.VMEM((ROWS, columns), low),
            pltpu.VMEM((8 * ROWS, HEAD_DIM), low),
            pltpu.VMEM((4, ROWS, columns), low),
            pltpu.VMEM((4, ROWS, columns), low),
            pltpu.VMEM((ROWS, columns), wide),
            pltpu.VMEM((8, ROWS, ROWS), wide),
            pltpu.VMEM((8, ROWS, ROWS), wide),
            pltpu.VMEM((ROWS, ROWS), wide),
            pltpu.VMEM((16, columns), wide),
            DMA((13,)),
            DMA((2,)),
            DMA((2, 8)),
            DMA((2,)),
            DMA((2,)),
            DMA((5,)),
            DMA((5,)),
            DMA,
            DMA((4,)),
            DMA,
            DMA,
            DMA((2,)),
            DMA((2, 8)),
            DMA((2,)),
            DMA((2,)),
            DMA((2,)),
            DMA((2,)),
        ]
        + [DMA] * 8,
        compiler_params=pltpu.CompilerParams(
            collective_id=0, has_side_effects=True, vmem_limit_bytes=56 * 1024 * 1024
        ),
        name="backward",
    )(queries, out_grad, keys, values, small, hidden)


def body(hidden_in, queries, keys, values, attn_out, out_grad, log_totals):
    delta = jnp.sum(
        (out_grad[0].astype(jnp.float32) * attn_out[0].astype(jnp.float32)).reshape(
            ROWS, HEADS, HEAD_DIM
        ),
        axis=2,
    )

    def by_unit(array):
        return array.reshape(ROWS, 8, 2, 2).transpose(2, 1, 3, 0).reshape(UNITS, 2, ROWS)

    small = jnp.concatenate(
        [by_unit(log_totals[0]), by_unit(delta), jnp.zeros((UNITS, 4, ROWS), jnp.float32)], axis=1
    )
    query_grad, key_grad, value_grad, weight_grad = backward(
        queries[0], out_grad[0], keys[0], values[0], small, hidden_in[0]
    )
    return (query_grad[None], key_grad[None], value_grad[None], weight_grad)


def solution(mesh):
    rows = P("dp", "seq", None)
    return jax.shard_map(
        body,
        mesh=mesh,
        in_specs=(rows,) * 7,
        out_specs=(rows, rows, rows, P(("seq", "dp"), None)),
        check_vma=False,
    )
```

```python
import functools

import jax
import jax.numpy as jnp
from jax import lax
from jax.experimental import pallas as pl
from jax.experimental.pallas import tpu as pltpu
from jax.sharding import PartitionSpec as P

HEADS = 32
KV_HEADS = 8
HEAD_DIM = 128
SCALE = HEAD_DIM ** (-0.5)
LOG2E = 1.4426950408889634
BLOCK = 512
ROWS = 128
UNITS = 16
NT = (((1,), (1,)), ((), ()))
TN = (((0,), (0,)), ((), ()))
NN = (((1,), (0,)), ((), ()))
RING = (4, 1, 7, 2, 6, 3, 5)
TURNS = tuple((flip, step) for step in (4, 1, 7, 2, 6, 3, 5, 0) for flip in (0, 1))[:-2] + ((1, 0),)
MESH = pl.DeviceIdType.MESH
ANY = pl.BlockSpec(memory_space=pl.ANY)
VMEM = pl.BlockSpec(memory_space=pltpu.VMEM)
DMA = pltpu.SemaphoreType.DMA


def place():
    seq = lax.axis_index("seq")
    unit = lax.rem(seq, UNITS)
    return seq, seq - unit, unit, unit // 8, lax.rem(unit, 8)


def send(src, dst, send_sem, recv_sem, **device):
    copy = pltpu.make_async_remote_copy(
        src_ref=src,
        dst_ref=dst,
        send_sem=send_sem,
        recv_sem=recv_sem,
        device_id=device,
        device_id_type=MESH,
    )
    copy.start()


def drain(ref, sem):
    pltpu.make_async_copy(ref, ref, sem).wait()


def rows_of(block):
    return pl.ds(pl.multiple_of(block * ROWS, ROWS), ROWS)


def columns_of(block, width=HEAD_DIM):
    return pl.ds(pl.multiple_of(block * width, width), width)


def scores_of(key, query, total):
    scores = lax.dot_general(key, query, NT, preferred_element_type=jnp.float32)
    return jnp.exp2(scores * (SCALE * LOG2E) - total)


def kernel(
    query_ref,
    grad_ref,
    key_ref,
    value_ref,
    output_ref,
    total_ref,
    hidden_ref,
    query_grad,
    key_grad,
    value_grad,
    weight_grad,
    query_unit,
    grad_unit,
    key_unit,
    value_unit,
    small_unit,
    hidden_unit,
    grad_own,
    output_own,
    total_own,
    small_own,
    probs_kept,
    query_part,
    key_sum,
    value_sum,
    low,
    halves,
    staged,
    value_own,
    value_in,
    summed,
    piece,
    piece_in,
    final,
    final_in,
    own_sem,
    front_send,
    front_recv,
    pass_send,
    pass_recv,
    bulk_send,
    bulk_recv,
    hidden_send,
    hidden_recv,
    core_send,
    core_recv,
    half_send,
    half_recv,
    ring_send,
    ring_recv,
    query_send,
    query_recv,
    gather_send,
    gather_recv,
    side_send,
    side_recv,
    piece_send,
    piece_recv,
    final_send,
    final_recv,
):
    seq, base, unit, half, lane = place()
    dp = lax.axis_index("dp")
    across = seq // 8
    twin = dp + 1 - 2 * lax.rem(dp, 2)
    partner = base + (1 - half) * 8 + lane

    def turned(flip, step):
        return (half + flip - 2 * half * flip) * 8 + lax.rem(lane + step, 8)

    barrier = pltpu.get_barrier_semaphore()
    for step in range(1, UNITS):
        pl.semaphore_signal(
            barrier,
            inc=1,
            device_id={"seq": base + lax.rem(unit + step, UNITS)},
            device_id_type=MESH,
        )
    for over in (2, 1, 3, 0):
        for step in range(8):
            if over or step:
                pl.semaphore_signal(
                    barrier,
                    inc=1,
                    device_id={
                        "seq": lax.rem(across + over, 4) * 8 + lane,
                        "dp": lax.rem(dp + step, 8),
                    },
                    device_id_type=MESH,
                )
    rows_own = (
        pltpu.make_async_copy(grad_ref, grad_own, own_sem.at[13]),
        pltpu.make_async_copy(output_ref, output_own, own_sem.at[14]),
        pltpu.make_async_copy(total_ref, total_own, own_sem.at[15]),
    )
    for copy in rows_own:
        copy.start()
    pl.semaphore_wait(barrier, 46)

    pairs = ((key_ref, key_unit), (value_ref, value_unit))
    for step in RING:
        target = lax.rem(lane + step, 8)
        for which, (source, landing) in enumerate(pairs):
            send(
                source.at[:, columns_of(target)],
                landing.at[rows_of(unit)],
                front_send.at[which],
                front_recv.at[which, lane],
                seq=base + half * 8 + target,
            )
    for which, (source, landing) in enumerate(pairs):
        send(
            source.at[:, columns_of(lane)],
            landing.at[rows_of(unit)],
            pass_send.at[which],
            pass_recv.at[which],
            seq=partner,
        )
    for over in (2, 1, 3):
        target = lax.rem(across + over, 4)
        send(
            hidden_ref.at[:, columns_of(target, 8 * ROWS)],
            hidden_unit.at[rows_of(across * 8 + dp)],
            side_send,
            side_recv.at[across],
            seq=target * 8 + lane,
        )

    def along(block, source, row):
        for step in (2, 1, 3):
            send(
                block,
                hidden_unit.at[row],
                hidden_send,
                hidden_recv.at[source, dp // 2],
                dp=lax.rem(dp + 2 * step, 8),
            )
        send(block, hidden_unit.at[row], core_send, core_recv, dp=twin)

    quarter = hidden_ref.at[:, columns_of(across, 8 * ROWS)]
    along(quarter, across, rows_of(across * 8 + dp))
    for head in range(2):
        for flip, step in TURNS:
            target = turned(flip, step)
            columns = columns_of(lax.rem(target, 8) * 4 + (target // 8) * 2 + head)
            for which, (source, landing) in enumerate(
                ((query_ref, query_unit), (grad_ref, grad_unit))
            ):
                send(
                    source.at[:, columns],
                    landing.at[head, rows_of(unit)],
                    bulk_send.at[head * 2 + which],
                    bulk_recv.at[head * 2 + which],
                    seq=base + target,
                )
    for copy in rows_own:
        copy.wait()
    column = lax.broadcasted_iota(jnp.int32, (ROWS, ROWS), 1)
    delta = jnp.zeros((ROWS, ROWS), jnp.float32)
    for head in range(HEADS):
        columns = slice(head * HEAD_DIM, (head + 1) * HEAD_DIM)
        row = jnp.sum(
            grad_own[:, columns].astype(jnp.float32) * output_own[:, columns].astype(jnp.float32),
            axis=1,
            keepdims=True,
        )
        delta = jnp.where(column == head, row, delta)
    delta = delta.T
    totals = total_own[...]
    for target in range(UNITS):
        head = (target % 8) * 4 + (target // 8) * 2
        small_own[target, 0:2, :] = totals[head : head + 2, :]
        small_own[target, 2:4, :] = delta[head : head + 2, :]
    for flip, step in TURNS:
        target = turned(flip, step)
        send(
            small_own.at[target],
            small_unit.at[unit],
            bulk_send.at[4],
            bulk_recv.at[4],
            seq=base + target,
        )
    small_unit[unit] = small_own[unit]
    mine = lane * 4 + half * 2
    own = (
        (key_ref.at[:, columns_of(lane)], key_unit.at[rows_of(unit)]),
        (value_ref.at[:, columns_of(lane)], value_unit.at[rows_of(unit)]),
        (query_ref.at[:, columns_of(mine)], query_unit.at[0, rows_of(unit)]),
        (grad_ref.at[:, columns_of(mine)], grad_unit.at[0, rows_of(unit)]),
        (query_ref.at[:, columns_of(mine + 1)], query_unit.at[1, rows_of(unit)]),
        (grad_ref.at[:, columns_of(mine + 1)], grad_unit.at[1, rows_of(unit)]),
        (quarter, hidden_unit.at[rows_of(across * 8 + dp)]),
    )
    own = [pltpu.make_async_copy(*pair, own_sem.at[i]) for i, pair in enumerate(own)]
    for copy in own:
        copy.start()
    for step in RING:
        source = lax.rem(lane - step + 8, 8)
        for which, (_, landing) in enumerate(pairs):
            block = landing.at[rows_of(half * 8 + source)]
            drain(block, front_recv.at[which, source])
            send(block, block, pass_send.at[which], pass_recv.at[which], seq=partner)

    for over in (1, 3, 2):
        source = lax.rem(across + over, 4)
        row = rows_of(source * 8 + dp)
        drain(hidden_unit.at[row], side_recv.at[source])
        along(hidden_unit.at[row], source, row)

    key_sum[...] = jnp.zeros_like(key_sum)
    value_sum[...] = jnp.zeros_like(value_sum)
    causal = lax.broadcasted_iota(jnp.int32, (BLOCK, BLOCK), 0) <= lax.broadcasted_iota(
        jnp.int32, (BLOCK, BLOCK), 1
    )
    per = BLOCK // ROWS
    positions = UNITS * ROWS // BLOCK

    def spread(position, row):
        return jnp.concatenate(
            [small_unit[position * per + t, row : row + 1, :] for t in range(per)], axis=1
        )

    def later(head, position, front, probs, query, grad, delta):
        fronts = pl.ds(front * BLOCK, BLOCK)
        key = key_unit[fronts, :]
        dprobs = lax.dot_general(
            value_unit[fronts, :], grad, NT, preferred_element_type=jnp.float32
        )
        dscores = (probs * (dprobs - delta)).astype(jnp.bfloat16)
        key_sum[fronts, :] += lax.dot_general(
            dscores, query, NN, preferred_element_type=jnp.float32
        )
        return lax.dot_general(dscores, key, TN, preferred_element_type=jnp.float32)

    def first(position, front, query, grad, total):
        fronts = pl.ds(front * BLOCK, BLOCK)
        probs = scores_of(key_unit[fronts, :], query, total)
        if front == position:
            probs = jnp.where(causal, probs, 0.0)
        value_sum[fronts, :] += lax.dot_general(
            probs.astype(jnp.bfloat16), grad, NN, preferred_element_type=jnp.float32
        )
        return probs

    def give_query(head):
        for flip, step in TURNS:
            target = turned(flip, step)
            send(
                query_part.at[head, rows_of(target)],
                query_grad.at[:, columns_of(mine + head)],
                query_send.at[head],
                query_recv.at[head],
                seq=base + target,
            )
        pltpu.make_async_copy(
            query_part.at[head, rows_of(unit)],
            query_grad.at[:, columns_of(mine + head)],
            own_sem.at[8 + head],
        ).start()

    for copy in own[:4]:
        copy.wait()
    for which, (_, landing) in enumerate(pairs):
        drain(landing.at[pl.ds(0, 8 * ROWS)], pass_recv.at[which])
    some = pl.ds(0, 15 * ROWS)
    drain(query_unit.at[0, some], bulk_recv.at[0])
    drain(grad_unit.at[0, some], bulk_recv.at[1])
    drain(small_unit.at[pl.ds(0, 15)], bulk_recv.at[4])
    for position in range(positions):
        rows = pl.ds(position * BLOCK, BLOCK)
        query = query_unit[0, rows, :]
        grad = grad_unit[0, rows, :]
        total = spread(position, 0) * LOG2E
        delta = spread(position, 2)
        query_sum = None
        for front in range(position + 1):
            probs = first(position, front, query, grad, total)
            term = later(0, position, front, probs, query, grad, delta)
            query_sum = term if query_sum is None else query_sum + term
        query_part[0, rows, :] = (query_sum * SCALE).astype(jnp.bfloat16)

    for copy in own[4:6]:
        copy.wait()
    drain(query_unit.at[1, some], bulk_recv.at[2])
    drain(grad_unit.at[1, some], bulk_recv.at[3])
    give_query(0)
    slot = 0
    for position in range(positions):
        rows = pl.ds(position * BLOCK, BLOCK)
        query = query_unit[1, rows, :]
        grad = grad_unit[1, rows, :]
        total = spread(position, 1) * LOG2E
        for front in range(position + 1):
            probs_kept[slot] = first(position, front, query, grad, total)
            slot += 1

    def give_half(which, array, factor):
        for step in RING + (0,):
            target = lax.rem(lane + step, 8)
            low[which, target] = (array[rows_of((1 - half) * 8 + target), :] * factor).astype(
                jnp.bfloat16
            )
            send(
                low.at[which, target],
                halves.at[which, target],
                half_send.at[which],
                half_recv.at[which, target],
                seq=partner,
            )

    def give_whole(which, array, factor, landing):
        landing = landing.at[:, columns_of(lane)]
        for step in RING + (0,):
            target = lax.rem(lane + step, 8)
            drain(halves.at[which, target], half_recv.at[which, target])
            staged[which, target] = (
                array[rows_of(half * 8 + target), :] * factor
                + halves[which, target].astype(jnp.float32)
            ).astype(jnp.bfloat16)
            if step:
                send(
                    staged.at[which, target],
                    landing,
                    ring_send.at[which],
                    ring_recv.at[which, lane],
                    seq=base + half * 8 + target,
                )
            else:
                pltpu.make_async_copy(
                    staged.at[which, target], landing, own_sem.at[10 + which]
                ).start()

    give_half(0, value_sum, 1.0)
    slot = 0
    for position in range(positions):
        rows = pl.ds(position * BLOCK, BLOCK)
        query = query_unit[1, rows, :]
        grad = grad_unit[1, rows, :]
        delta = spread(position, 3)
        query_sum = None
        for front in range(position + 1):
            term = later(1, position, front, probs_kept[slot], query, grad, delta)
            query_sum = term if query_sum is None else query_sum + term
            slot += 1
        query_part[1, rows, :] = (query_sum * SCALE).astype(jnp.bfloat16)
    give_half(1, key_sum, SCALE)
    give_whole(0, value_sum, 1.0, value_own)
    give_query(1)
    for over in range(4):
        for step in (1, 3, 2):
            source = lax.rem(dp + 2 * step, 8)
            arrived = hidden_unit.at[rows_of(over * 8 + source)]
            drain(arrived, hidden_recv.at[over, source // 2])
            send(arrived, arrived, core_send, core_recv, dp=twin)

    for step in (0,) + RING:
        group = lax.rem(lane - step + 8, 8)
        block = value_own.at[:, columns_of(group)]
        if step:
            drain(staged.at[0, 0], ring_recv.at[0, group])
        else:
            drain(staged.at[0, 0], own_sem.at[10])

        def give_block(over):
            send(
                block,
                value_in.at[rows_of(across * 8 + dp)],
                gather_send,
                gather_recv.at[across],
                seq=lax.rem(across + over, 4) * 8 + lane,
                dp=group,
            )

        for over in (2, 1, 3):
            give_block(over)
        pl.when(group != dp)(functools.partial(give_block, 0))

    pltpu.make_async_copy(value_own, value_grad, own_sem.at[12]).start()
    value_in[rows_of(across * 8 + dp), :] = value_own[:, columns_of(dp)]
    give_whole(1, key_sum, SCALE, key_grad)
    own[6].wait()
    drain(hidden_unit.at[pl.ds(0, 16 * ROWS)], core_recv)
    for over in (0, 1, 3, 2):
        source = lax.rem(across + over, 4)
        drain(value_in.at[pl.ds(0, (8 if over else 7) * ROWS)], gather_recv.at[source])
        rows = pl.ds(pl.multiple_of(source * 8 * ROWS, 8 * ROWS), 8 * ROWS)
        total = lax.dot_general(
            value_in[rows, :], hidden_unit[rows, :], TN, preferred_element_type=jnp.float32
        )
        if over == 0:
            summed[...] = total
        else:
            summed[...] += total
    for step in RING:
        target = lax.rem(lane + step, 8)
        piece[target] = summed[:, columns_of(target)].astype(jnp.bfloat16)
        send(piece.at[target], piece_in.at[lane], piece_send, piece_recv, seq=across * 8 + target)
    final[...] = summed[:, columns_of(lane)]
    drain(piece.at[pl.ds(0, 7)], piece_recv)
    total = final[...]
    for step in range(1, 8):
        total = total + piece_in[lax.rem(lane + step, 8)].astype(jnp.float32)
    final[...] = total.T
    for step in range(1, 8):
        target = lax.rem(dp + step, 8)
        send(
            final.at[pl.ds(pl.multiple_of(target * 16, 16), 16)],
            final_in.at[:, columns_of(dp)],
            final_send,
            final_recv,
            dp=target,
        )
    final_in[:, columns_of(dp)] = final[pl.ds(pl.multiple_of(dp * 16, 16), 16), :]
    drain(final.at[pl.ds(0, 7 * 16)], final_recv)
    weight_grad[...] = final_in[...]

    for which, (_, landing) in enumerate(pairs):
        drain(landing.at[pl.ds(0, 7 * ROWS)], front_send.at[which])
        drain(landing.at[pl.ds(0, 8 * ROWS)], pass_send.at[which])
    for which in range(4):
        drain(query_unit.at[0, some], bulk_send.at[which])
    drain(small_unit.at[pl.ds(0, 15)], bulk_send.at[4])
    drain(hidden_unit.at[pl.ds(0, 3 * ROWS)], side_send)
    drain(hidden_unit.at[pl.ds(0, 12 * ROWS)], hidden_send)
    drain(hidden_unit.at[pl.ds(0, 16 * ROWS)], core_send)
    drain(staged.at[1, 0], own_sem.at[11])
    drain(value_own, own_sem.at[12])
    for step in RING:
        drain(staged.at[1, 0], ring_recv.at[1, lax.rem(lane - step + 8, 8)])
    for head in range(2):
        drain(query_part.at[head, rows_of(0)], own_sem.at[8 + head])
        drain(query_part.at[head, some], query_recv.at[head])
        drain(query_part.at[head, some], query_send.at[head])
    for which in range(2):
        drain(halves.at[which], half_send.at[which])
        drain(staged.at[which, pl.ds(0, 7)], ring_send.at[which])
    drain(value_in.at[pl.ds(0, 31 * ROWS)], gather_send)
    drain(piece.at[pl.ds(0, 7)], piece_send)
    drain(final.at[pl.ds(0, 7 * 16)], final_send)


def backward(queries, out_grad, keys, values, attn_out, log_totals, hidden):
    low = jnp.bfloat16
    wide = jnp.float32
    columns = KV_HEADS * HEAD_DIM
    length = UNITS * ROWS
    positions = length // BLOCK
    slots = positions * (positions + 1) // 2
    return pl.pallas_call(
        kernel,
        out_shape=(
            jax.ShapeDtypeStruct((ROWS, HEADS * HEAD_DIM), low),
            jax.ShapeDtypeStruct((ROWS, columns), low),
            jax.ShapeDtypeStruct((ROWS, columns), low),
            jax.ShapeDtypeStruct((16, columns), wide),
        ),
        in_specs=[ANY] * 7,
        out_specs=(ANY, ANY, ANY, VMEM),
        scratch_shapes=[
            pltpu.VMEM((2, length, HEAD_DIM), low),
            pltpu.VMEM((2, length, HEAD_DIM), low),
            pltpu.VMEM((length, HEAD_DIM), low),
            pltpu.VMEM((length, HEAD_DIM), low),
            pltpu.VMEM((UNITS, 4, ROWS), wide),
            pltpu.VMEM((4 * 8 * ROWS, 8 * ROWS), low),
            pltpu.VMEM((ROWS, HEADS * HEAD_DIM), low),
            pltpu.VMEM((ROWS, HEADS * HEAD_DIM), low),
            pltpu.VMEM((HEADS, ROWS), wide),
            pltpu.VMEM((UNITS, 4, ROWS), wide),
            pltpu.VMEM((slots, BLOCK, BLOCK), wide),
            pltpu.VMEM((2, length, HEAD_DIM), low),
            pltpu.VMEM((length, HEAD_DIM), wide),
            pltpu.VMEM((length, HEAD_DIM), wide),
            pltpu.VMEM((2, 8, ROWS, HEAD_DIM), low),
            pltpu.VMEM((2, 8, ROWS, HEAD_DIM), low),
            pltpu.VMEM((2, 8, ROWS, HEAD_DIM), low),
            pltpu.VMEM((ROWS, columns), low),
            pltpu.VMEM((4 * 8 * ROWS, HEAD_DIM), low),
            pltpu.VMEM((ROWS, 8 * ROWS), wide),
            pltpu.VMEM((8, ROWS, ROWS), low),
            pltpu.VMEM((8, ROWS, ROWS), low),
            pltpu.VMEM((ROWS, ROWS), wide),
            pltpu.VMEM((16, columns), wide),
            DMA((16,)),
            DMA((2,)),
            DMA((2, 8)),
            DMA((2,)),
            DMA((2,)),
            DMA((5,)),
            DMA((5,)),
            DMA,
            DMA((4, 4)),
            DMA,
            DMA,
            DMA((2,)),
            DMA((2, 8)),
            DMA((2,)),
            DMA((2, 8)),
            DMA((2,)),
            DMA((2,)),
        ]
        + [DMA, DMA((4,)), DMA, DMA((4,)), DMA, DMA, DMA, DMA],
        compiler_params=pltpu.CompilerParams(
            collective_id=0, has_side_effects=True, vmem_limit_bytes=56 * 1024 * 1024
        ),
        name="backward",
    )(queries, out_grad, keys, values, attn_out, log_totals, hidden)


def settle_kernel(*refs):
    sources, results, held, come, go = refs[:4], refs[4:8], refs[8:12], refs[12], refs[13]
    pieces = [(0, pl.ds(32 * i, 32)) for i in range(4)]
    pieces += [(i, pl.ds(0, sources[i].shape[0])) for i in range(1, 4)]
    loads = [
        pltpu.make_async_copy(sources[i].at[rows], held[i].at[rows], come.at[n])
        for n, (i, rows) in enumerate(pieces)
    ]
    stores = [
        pltpu.make_async_copy(held[i].at[rows], results[i].at[rows], go.at[n])
        for n, (i, rows) in enumerate(pieces)
    ]
    for load in loads:
        load.start()
    for load, store in zip(loads, stores):
        load.wait()
        store.start()
    for store in stores:
        store.wait()


def settle(*arrays):
    return pl.pallas_call(
        settle_kernel,
        out_shape=tuple(jax.ShapeDtypeStruct(array.shape, array.dtype) for array in arrays),
        in_specs=[ANY] * 4,
        out_specs=(ANY,) * 4,
        scratch_shapes=[pltpu.VMEM(array.shape, array.dtype) for array in arrays]
        + [DMA((7,)), DMA((7,))],
        name="settle",
    )(*arrays)


def body(hidden_in, queries, keys, values, attn_out, out_grad, log_totals):
    query_grad, key_grad, value_grad, weight_grad = settle(
        *backward(
            queries[0],
            out_grad[0],
            keys[0],
            values[0],
            attn_out[0],
            log_totals[0].T,
            hidden_in[0],
        )
    )
    return (query_grad[None], key_grad[None], value_grad[None], weight_grad)


def solution(mesh):
    rows = P("dp", "seq", None)
    return jax.shard_map(
        body,
        mesh=mesh,
        in_specs=(rows,) * 7,
        out_specs=(rows, rows, rows, P(("seq", "dp"), None)),
        check_vma=False,
    )
```

```python
import functools

import jax
import jax.numpy as jnp
from jax import lax
from jax.experimental import pallas as pl
from jax.experimental.pallas import tpu as pltpu
from jax.sharding import PartitionSpec as P

HEADS = 32
KV_HEADS = 8
HEAD_DIM = 128
SCALE = HEAD_DIM ** (-0.5)
LOG2E = 1.4426950408889634
BLOCK = 512
ROWS = 128
UNITS = 16
NT = (((1,), (1,)), ((), ()))
TN = (((0,), (0,)), ((), ()))
NN = (((1,), (0,)), ((), ()))
RING = (4, 1, 7, 2, 6, 3, 5)
TURNS = tuple((flip, step) for step in (4, 1, 7, 2, 6, 3, 5, 0) for flip in (0, 1))[:-2] + ((1, 0),)
MESH = pl.DeviceIdType.MESH
ANY = pl.BlockSpec(memory_space=pl.ANY)
VMEM = pl.BlockSpec(memory_space=pltpu.VMEM)
DMA = pltpu.SemaphoreType.DMA


def place():
    seq = lax.axis_index("seq")
    unit = lax.rem(seq, UNITS)
    return seq, seq - unit, unit, unit // 8, lax.rem(unit, 8)


def send(src, dst, send_sem, recv_sem, **device):
    copy = pltpu.make_async_remote_copy(
        src_ref=src,
        dst_ref=dst,
        send_sem=send_sem,
        recv_sem=recv_sem,
        device_id=device,
        device_id_type=MESH,
    )
    copy.start()


def drain(ref, sem):
    pltpu.make_async_copy(ref, ref, sem).wait()


def rows_of(block):
    return pl.ds(pl.multiple_of(block * ROWS, ROWS), ROWS)


def columns_of(block, width=HEAD_DIM):
    return pl.ds(pl.multiple_of(block * width, width), width)


def scores_of(key, query, total):
    scores = lax.dot_general(key, query, NT, preferred_element_type=jnp.float32)
    return jnp.exp2(scores * (SCALE * LOG2E) - total)


def kernel(
    query_ref,
    grad_ref,
    key_ref,
    value_ref,
    output_ref,
    total_ref,
    hidden_ref,
    query_grad,
    key_grad,
    value_grad,
    weight_grad,
    query_unit,
    grad_unit,
    key_unit,
    value_unit,
    small_unit,
    hidden_unit,
    grad_own,
    output_own,
    total_own,
    small_own,
    probs_kept,
    query_part,
    key_sum,
    value_sum,
    low,
    halves,
    staged,
    value_own,
    value_in,
    summed,
    piece,
    piece_in,
    final,
    final_in,
    own_sem,
    front_send,
    front_recv,
    pass_send,
    pass_recv,
    bulk_send,
    bulk_recv,
    hidden_send,
    hidden_recv,
    core_send,
    core_recv,
    half_send,
    half_recv,
    ring_send,
    ring_recv,
    query_send,
    query_recv,
    gather_send,
    gather_recv,
    side_send,
    side_recv,
    piece_send,
    piece_recv,
    final_send,
    final_recv,
):
    seq, base, unit, half, lane = place()
    dp = lax.axis_index("dp")
    across = seq // 8
    twin = dp + 1 - 2 * lax.rem(dp, 2)
    partner = base + (1 - half) * 8 + lane

    def turned(flip, step):
        return (half + flip - 2 * half * flip) * 8 + lax.rem(lane + step, 8)

    barrier = pltpu.get_barrier_semaphore()
    for step in range(1, UNITS):
        pl.semaphore_signal(
            barrier,
            inc=1,
            device_id={"seq": base + lax.rem(unit + step, UNITS)},
            device_id_type=MESH,
        )
    for over in (2, 1, 3, 0):
        for step in range(8):
            if over or step:
                pl.semaphore_signal(
                    barrier,
                    inc=1,
                    device_id={
                        "seq": lax.rem(across + over, 4) * 8 + lane,
                        "dp": lax.rem(dp + step, 8),
                    },
                    device_id_type=MESH,
                )
    rows_own = (
        pltpu.make_async_copy(grad_ref, grad_own, own_sem.at[13]),
        pltpu.make_async_copy(output_ref, output_own, own_sem.at[14]),
        pltpu.make_async_copy(total_ref, total_own, own_sem.at[15]),
    )
    for copy in rows_own:
        copy.start()
    pl.semaphore_wait(barrier, 46)

    pairs = ((key_ref, key_unit), (value_ref, value_unit))
    for step in RING:
        target = lax.rem(lane + step, 8)
        for which, (source, landing) in enumerate(pairs):
            send(
                source.at[:, columns_of(target)],
                landing.at[rows_of(unit)],
                front_send.at[which],
                front_recv.at[which, lane],
                seq=base + half * 8 + target,
            )
    for which, (source, landing) in enumerate(pairs):
        send(
            source.at[:, columns_of(lane)],
            landing.at[rows_of(unit)],
            pass_send.at[which],
            pass_recv.at[which],
            seq=partner,
        )
    for over in (2, 1, 3):
        target = lax.rem(across + over, 4)
        send(
            hidden_ref.at[:, columns_of(target, 8 * ROWS)],
            hidden_unit.at[rows_of(across * 8 + dp)],
            side_send,
            side_recv.at[across],
            seq=target * 8 + lane,
        )

    def along(block, source, row):
        for step in (2, 1, 3):
            send(
                block,
                hidden_unit.at[row],
                hidden_send,
                hidden_recv.at[source, dp // 2],
                dp=lax.rem(dp + 2 * step, 8),
            )
        send(block, hidden_unit.at[row], core_send, core_recv, dp=twin)

    quarter = hidden_ref.at[:, columns_of(across, 8 * ROWS)]
    along(quarter, across, rows_of(across * 8 + dp))
    for head in range(2):
        for flip, step in TURNS:
            target = turned(flip, step)
            columns = columns_of(lax.rem(target, 8) * 4 + (target // 8) * 2 + head)
            for which, (source, landing) in enumerate(
                ((query_ref, query_unit), (grad_ref, grad_unit))
            ):
                send(
                    source.at[:, columns],
                    landing.at[head, rows_of(unit)],
                    bulk_send.at[head * 2 + which],
                    bulk_recv.at[head * 2 + which],
                    seq=base + target,
                )
    for copy in rows_own:
        copy.wait()
    column = lax.broadcasted_iota(jnp.int32, (ROWS, ROWS), 1)
    delta = jnp.zeros((ROWS, ROWS), jnp.float32)
    for head in range(HEADS):
        columns = slice(head * HEAD_DIM, (head + 1) * HEAD_DIM)
        row = jnp.sum(
            grad_own[:, columns].astype(jnp.float32) * output_own[:, columns].astype(jnp.float32),
            axis=1,
            keepdims=True,
        )
        delta = jnp.where(column == head, row, delta)
    delta = delta.T
    totals = total_own[...]
    for target in range(UNITS):
        head = (target % 8) * 4 + (target // 8) * 2
        small_own[target, 0:2, :] = totals[head : head + 2, :]
        small_own[target, 2:4, :] = delta[head : head + 2, :]
    for flip, step in TURNS:
        target = turned(flip, step)
        send(
            small_own.at[target],
            small_unit.at[unit],
            bulk_send.at[4],
            bulk_recv.at[4],
            seq=base + target,
        )
    small_unit[unit] = small_own[unit]
    mine = lane * 4 + half * 2
    own = (
        (key_ref.at[:, columns_of(lane)], key_unit.at[rows_of(unit)]),
        (value_ref.at[:, columns_of(lane)], value_unit.at[rows_of(unit)]),
        (query_ref.at[:, columns_of(mine)], query_unit.at[0, rows_of(unit)]),
        (grad_ref.at[:, columns_of(mine)], grad_unit.at[0, rows_of(unit)]),
        (query_ref.at[:, columns_of(mine + 1)], query_unit.at[1, rows_of(unit)]),
        (grad_ref.at[:, columns_of(mine + 1)], grad_unit.at[1, rows_of(unit)]),
        (quarter, hidden_unit.at[rows_of(across * 8 + dp)]),
    )
    own = [pltpu.make_async_copy(*pair, own_sem.at[i]) for i, pair in enumerate(own)]
    for copy in own:
        copy.start()
    for step in RING:
        source = lax.rem(lane - step + 8, 8)
        for which, (_, landing) in enumerate(pairs):
            block = landing.at[rows_of(half * 8 + source)]
            drain(block, front_recv.at[which, source])
            send(block, block, pass_send.at[which], pass_recv.at[which], seq=partner)

    for over in (1, 3, 2):
        source = lax.rem(across + over, 4)
        row = rows_of(source * 8 + dp)
        drain(hidden_unit.at[row], side_recv.at[source])
        along(hidden_unit.at[row], source, row)

    key_sum[...] = jnp.zeros_like(key_sum)
    value_sum[...] = jnp.zeros_like(value_sum)
    causal = lax.broadcasted_iota(jnp.int32, (BLOCK, BLOCK), 0) <= lax.broadcasted_iota(
        jnp.int32, (BLOCK, BLOCK), 1
    )
    per = BLOCK // ROWS
    positions = UNITS * ROWS // BLOCK

    def spread(position, row):
        return jnp.concatenate(
            [small_unit[position * per + t, row : row + 1, :] for t in range(per)], axis=1
        )

    def later(head, position, front, probs, query, grad, delta):
        fronts = pl.ds(front * BLOCK, BLOCK)
        key = key_unit[fronts, :]
        dprobs = lax.dot_general(
            value_unit[fronts, :], grad, NT, preferred_element_type=jnp.float32
        )
        dscores = (probs * (dprobs - delta)).astype(jnp.bfloat16)
        key_sum[fronts, :] += lax.dot_general(
            dscores, query, NN, preferred_element_type=jnp.float32
        )
        return lax.dot_general(dscores, key, TN, preferred_element_type=jnp.float32)

    def first(position, front, query, grad, total):
        fronts = pl.ds(front * BLOCK, BLOCK)
        probs = scores_of(key_unit[fronts, :], query, total)
        if front == position:
            probs = jnp.where(causal, probs, 0.0)
        value_sum[fronts, :] += lax.dot_general(
            probs.astype(jnp.bfloat16), grad, NN, preferred_element_type=jnp.float32
        )
        return probs

    def give_query(head):
        for flip, step in TURNS:
            target = turned(flip, step)
            send(
                query_part.at[head, rows_of(target)],
                query_grad.at[:, columns_of(mine + head)],
                query_send.at[head],
                query_recv.at[head],
                seq=base + target,
            )
        pltpu.make_async_copy(
            query_part.at[head, rows_of(unit)],
            query_grad.at[:, columns_of(mine + head)],
            own_sem.at[8 + head],
        ).start()

    for copy in own[:4]:
        copy.wait()
    for which, (_, landing) in enumerate(pairs):
        drain(landing.at[pl.ds(0, 8 * ROWS)], pass_recv.at[which])
    some = pl.ds(0, 15 * ROWS)
    drain(query_unit.at[0, some], bulk_recv.at[0])
    drain(grad_unit.at[0, some], bulk_recv.at[1])
    drain(small_unit.at[pl.ds(0, 15)], bulk_recv.at[4])
    for position in range(positions):
        rows = pl.ds(position * BLOCK, BLOCK)
        query = query_unit[0, rows, :]
        grad = grad_unit[0, rows, :]
        total = spread(position, 0) * LOG2E
        delta = spread(position, 2)
        query_sum = None
        for front in range(position + 1):
            probs = first(position, front, query, grad, total)
            term = later(0, position, front, probs, query, grad, delta)
            query_sum = term if query_sum is None else query_sum + term
        query_part[0, rows, :] = (query_sum * SCALE).astype(jnp.bfloat16)

    for copy in own[4:6]:
        copy.wait()
    drain(query_unit.at[1, some], bulk_recv.at[2])
    drain(grad_unit.at[1, some], bulk_recv.at[3])
    give_query(0)
    slot = 0
    for position in range(positions):
        rows = pl.ds(position * BLOCK, BLOCK)
        query = query_unit[1, rows, :]
        grad = grad_unit[1, rows, :]
        total = spread(position, 1) * LOG2E
        for front in range(position + 1):
            probs_kept[slot] = first(position, front, query, grad, total)
            slot += 1

    def give_half(which, array, factor):
        for step in RING + (0,):
            target = lax.rem(lane + step, 8)
            low[which, target] = (array[rows_of((1 - half) * 8 + target), :] * factor).astype(
                jnp.bfloat16
            )
            send(
                low.at[which, target],
                halves.at[which, target],
                half_send.at[which],
                half_recv.at[which, target],
                seq=partner,
            )

    def give_whole(which, array, factor, landing):
        landing = landing.at[:, columns_of(lane)]
        for step in RING + (0,):
            target = lax.rem(lane + step, 8)
            drain(halves.at[which, target], half_recv.at[which, target])
            staged[which, target] = (
                array[rows_of(half * 8 + target), :] * factor
                + halves[which, target].astype(jnp.float32)
            ).astype(jnp.bfloat16)
            if step:
                send(
                    staged.at[which, target],
                    landing,
                    ring_send.at[which],
                    ring_recv.at[which, lane],
                    seq=base + half * 8 + target,
                )
            else:
                pltpu.make_async_copy(
                    staged.at[which, target], landing, own_sem.at[10 + which]
                ).start()

    give_half(0, value_sum, 1.0)
    slot = 0
    for position in range(positions):
        rows = pl.ds(position * BLOCK, BLOCK)
        query = query_unit[1, rows, :]
        grad = grad_unit[1, rows, :]
        delta = spread(position, 3)
        query_sum = None
        for front in range(position + 1):
            term = later(1, position, front, probs_kept[slot], query, grad, delta)
            query_sum = term if query_sum is None else query_sum + term
            slot += 1
        query_part[1, rows, :] = (query_sum * SCALE).astype(jnp.bfloat16)
    give_half(1, key_sum, SCALE)
    give_whole(0, value_sum, 1.0, value_own)
    give_query(1)
    for over in range(4):
        for step in (1, 3, 2):
            source = lax.rem(dp + 2 * step, 8)
            arrived = hidden_unit.at[rows_of(over * 8 + source)]
            drain(arrived, hidden_recv.at[over, source // 2])
            send(arrived, arrived, core_send, core_recv, dp=twin)

    for step in (0,) + RING:
        group = lax.rem(lane - step + 8, 8)
        block = value_own.at[:, columns_of(group)]
        if step:
            drain(staged.at[0, 0], ring_recv.at[0, group])
        else:
            drain(staged.at[0, 0], own_sem.at[10])

        def give_block(over):
            send(
                block,
                value_in.at[rows_of(across * 8 + dp)],
                gather_send,
                gather_recv.at[across],
                seq=lax.rem(across + over, 4) * 8 + lane,
                dp=group,
            )

        for over in (2, 1, 3):
            give_block(over)
        pl.when(group != dp)(functools.partial(give_block, 0))

    pltpu.make_async_copy(value_own, value_grad, own_sem.at[12]).start()
    value_in[rows_of(across * 8 + dp), :] = value_own[:, columns_of(dp)]
    give_whole(1, key_sum, SCALE, key_grad)
    own[6].wait()
    drain(hidden_unit.at[pl.ds(0, 16 * ROWS)], core_recv)
    for over in (0, 1, 3, 2):
        source = lax.rem(across + over, 4)
        drain(value_in.at[pl.ds(0, (8 if over else 7) * ROWS)], gather_recv.at[source])
        rows = pl.ds(pl.multiple_of(source * 8 * ROWS, 8 * ROWS), 8 * ROWS)
        if over != 2:
            total = lax.dot_general(
                value_in[rows, :], hidden_unit[rows, :], TN, preferred_element_type=jnp.float32
            )
            if over == 0:
                summed[...] = total
            else:
                summed[...] += total
        else:
            for turn, part in enumerate((1 - lane // 4, lane // 4)):
                wide = columns_of(part, 4 * ROWS)
                summed[:, wide] += lax.dot_general(
                    value_in[rows, :],
                    hidden_unit[rows, wide],
                    TN,
                    preferred_element_type=jnp.float32,
                )
                for step in range(4):
                    if turn == 0 or step:
                        target = part * 4 + lax.rem(lane + step, 4)
                        piece[target] = summed[:, columns_of(target)].astype(jnp.bfloat16)
                        send(
                            piece.at[target],
                            piece_in.at[lane],
                            piece_send,
                            piece_recv,
                            seq=across * 8 + target,
                        )
    final[...] = summed[:, columns_of(lane)]
    drain(piece.at[pl.ds(0, 7)], piece_recv)
    total = final[...]
    for step in range(1, 8):
        total = total + piece_in[lax.rem(lane + step, 8)].astype(jnp.float32)
    final[...] = total.T
    for step in range(1, 8):
        target = lax.rem(dp + step, 8)
        send(
            final.at[pl.ds(pl.multiple_of(target * 16, 16), 16)],
            final_in.at[:, columns_of(dp)],
            final_send,
            final_recv,
            dp=target,
        )
    final_in[:, columns_of(dp)] = final[pl.ds(pl.multiple_of(dp * 16, 16), 16), :]
    drain(final.at[pl.ds(0, 7 * 16)], final_recv)
    weight_grad[...] = final_in[...]

    for which, (_, landing) in enumerate(pairs):
        drain(landing.at[pl.ds(0, 7 * ROWS)], front_send.at[which])
        drain(landing.at[pl.ds(0, 8 * ROWS)], pass_send.at[which])
    for which in range(4):
        drain(query_unit.at[0, some], bulk_send.at[which])
    drain(small_unit.at[pl.ds(0, 15)], bulk_send.at[4])
    drain(hidden_unit.at[pl.ds(0, 3 * ROWS)], side_send)
    drain(hidden_unit.at[pl.ds(0, 12 * ROWS)], hidden_send)
    drain(hidden_unit.at[pl.ds(0, 16 * ROWS)], core_send)
    drain(staged.at[1, 0], own_sem.at[11])
    drain(value_own, own_sem.at[12])
    for step in RING:
        drain(staged.at[1, 0], ring_recv.at[1, lax.rem(lane - step + 8, 8)])
    for head in range(2):
        drain(query_part.at[head, rows_of(0)], own_sem.at[8 + head])
        drain(query_part.at[head, some], query_recv.at[head])
        drain(query_part.at[head, some], query_send.at[head])
    for which in range(2):
        drain(halves.at[which], half_send.at[which])
        drain(staged.at[which, pl.ds(0, 7)], ring_send.at[which])
    drain(value_in.at[pl.ds(0, 31 * ROWS)], gather_send)
    drain(piece.at[pl.ds(0, 7)], piece_send)
    drain(final.at[pl.ds(0, 7 * 16)], final_send)


def backward(queries, out_grad, keys, values, attn_out, log_totals, hidden):
    low = jnp.bfloat16
    wide = jnp.float32
    columns = KV_HEADS * HEAD_DIM
    length = UNITS * ROWS
    positions = length // BLOCK
    slots = positions * (positions + 1) // 2
    return pl.pallas_call(
        kernel,
        out_shape=(
            jax.ShapeDtypeStruct((ROWS, HEADS * HEAD_DIM), low),
            jax.ShapeDtypeStruct((ROWS, columns), low),
            jax.ShapeDtypeStruct((ROWS, columns), low),
            jax.ShapeDtypeStruct((16, columns), wide),
        ),
        in_specs=[ANY] * 7,
        out_specs=(ANY, ANY, ANY, VMEM),
        scratch_shapes=[
            pltpu.VMEM((2, length, HEAD_DIM), low),
            pltpu.VMEM((2, length, HEAD_DIM), low),
            pltpu.VMEM((length, HEAD_DIM), low),
            pltpu.VMEM((length, HEAD_DIM), low),
            pltpu.VMEM((UNITS, 4, ROWS), wide),
            pltpu.VMEM((4 * 8 * ROWS, 8 * ROWS), low),
            pltpu.VMEM((ROWS, HEADS * HEAD_DIM), low),
            pltpu.VMEM((ROWS, HEADS * HEAD_DIM), low),
            pltpu.VMEM((HEADS, ROWS), wide),
            pltpu.VMEM((UNITS, 4, ROWS), wide),
            pltpu.VMEM((slots, BLOCK, BLOCK), wide),
            pltpu.VMEM((2, length, HEAD_DIM), low),
            pltpu.VMEM((length, HEAD_DIM), wide),
            pltpu.VMEM((length, HEAD_DIM), wide),
            pltpu.VMEM((2, 8, ROWS, HEAD_DIM), low),
            pltpu.VMEM((2, 8, ROWS, HEAD_DIM), low),
            pltpu.VMEM((2, 8, ROWS, HEAD_DIM), low),
            pltpu.VMEM((ROWS, columns), low),
            pltpu.VMEM((4 * 8 * ROWS, HEAD_DIM), low),
            pltpu.VMEM((ROWS, 8 * ROWS), wide),
            pltpu.VMEM((8, ROWS, ROWS), low),
            pltpu.VMEM((8, ROWS, ROWS), low),
            pltpu.VMEM((ROWS, ROWS), wide),
            pltpu.VMEM((16, columns), wide),
            DMA((16,)),
            DMA((2,)),
            DMA((2, 8)),
            DMA((2,)),
            DMA((2,)),
            DMA((5,)),
            DMA((5,)),
            DMA,
            DMA((4, 4)),
            DMA,
            DMA,
            DMA((2,)),
            DMA((2, 8)),
            DMA((2,)),
            DMA((2, 8)),
            DMA((2,)),
            DMA((2,)),
        ]
        + [DMA, DMA((4,)), DMA, DMA((4,)), DMA, DMA, DMA, DMA],
        compiler_params=pltpu.CompilerParams(
            collective_id=0, has_side_effects=True, vmem_limit_bytes=56 * 1024 * 1024
        ),
        name="backward",
    )(queries, out_grad, keys, values, attn_out, log_totals, hidden)


def settle_kernel(*refs):
    sources, results, held, come, go = refs[:4], refs[4:8], refs[8:12], refs[12], refs[13]
    pieces = [(0, pl.ds(32 * i, 32)) for i in range(4)]
    pieces += [(i, pl.ds(0, sources[i].shape[0])) for i in range(1, 4)]
    loads = [
        pltpu.make_async_copy(sources[i].at[rows], held[i].at[rows], come.at[n])
        for n, (i, rows) in enumerate(pieces)
    ]
    stores = [
        pltpu.make_async_copy(held[i].at[rows], results[i].at[rows], go.at[n])
        for n, (i, rows) in enumerate(pieces)
    ]
    for load in loads:
        load.start()
    for load, store in zip(loads, stores):
        load.wait()
        store.start()
    for store in stores:
        store.wait()


def settle(*arrays):
    return pl.pallas_call(
        settle_kernel,
        out_shape=tuple(jax.ShapeDtypeStruct(array.shape, array.dtype) for array in arrays),
        in_specs=[ANY] * 4,
        out_specs=(ANY,) * 4,
        scratch_shapes=[pltpu.VMEM(array.shape, array.dtype) for array in arrays]
        + [DMA((7,)), DMA((7,))],
        name="settle",
    )(*arrays)


def body(hidden_in, queries, keys, values, attn_out, out_grad, log_totals):
    query_grad, key_grad, value_grad, weight_grad = settle(
        *backward(
            queries[0],
            out_grad[0],
            keys[0],
            values[0],
            attn_out[0],
            log_totals[0].T,
            hidden_in[0],
        )
    )
    return (query_grad[None], key_grad[None], value_grad[None], weight_grad)


def solution(mesh):
    rows = P("dp", "seq", None)
    return jax.shard_map(
        body,
        mesh=mesh,
        in_specs=(rows,) * 7,
        out_specs=(rows, rows, rows, P(("seq", "dp"), None)),
        check_vma=False,
    )
```
